256 devices in a mesh: dp: 16 (over y, x_hi, core), mp: 16 (over z, x_lo).
Axes of the slice: x: 4 (x_hi: 2, x_lo: 2; x = x_hi * 2 + x_lo), y: 4, z: 8, core: 2. Of those that a mesh axis runs over, the one named last changes fastest.
Arguments:
- tokens: bfloat16 [8192, 6144], P('dp', 'mp'), may hold values from -6 to 6
- ln_gain: float32 [6144], replicated, may hold values from 0.1 to 1.9
- projected: bfloat16 [8192, 3, 4096], P('dp', None, 'mp'), may hold values from -12.5 to 12.5, as said below
- out_grad: bfloat16 [8192, 4096], P('dp', 'mp'), may hold values from -24 to 24
- w_joined: bfloat16 [6144, 3, 4096], P(None, None, 'mp'), may hold values from -0.078125 to 0.078125
Outputs:
- grad_weight: float32 [6144, 3, 4096], P('dp', None, 'mp')
- grad_input: bfloat16 [8192, 6144], P('dp', 'mp')
The draws below stay inside these ranges and needn't reach their ends.
Inputs may be any that keep to these rules, and one draw needn't show every extreme that they name: `projected`: each token's query, key and value projections, heads in order.
All inputs are finite; a program needn't handle non-finite values.
Results may differ from the reference program's by a relative error of at most 0.017.
Values may be sent and summed in bfloat16 or wider, within the bound.
A program may use at most 192 MiB of HBM per device.

```python
import jax
import jax.numpy as jnp
from jax import lax

D = 6144
HEADS = 32
HDIM = 128
SEQ = 512
HH = 4096
TOKENS = 8192


def draw_projected(key, part):
    key = jax.random.fold_in(key, 11)
    key_base = jax.random.fold_in(key, 0)
    images = TOKENS // SEQ
    width = HEADS * HDIM
    drawn = jnp.clip(jax.random.normal(key_base, (images, SEQ, 3, width), jnp.float32), -6.0, 6.0)
    return drawn.reshape(TOKENS, 3, width).astype(jnp.bfloat16)


def steps_of(key, shape, shards, low, largest):
    gain = 1.0
    for position, shards_of in shards:
        heights = jax.random.uniform(jax.random.fold_in(jax.random.fold_in(key, 6), position), (shards_of,), jnp.float32, low / len(shards), largest / len(shards))
        gain = gain * jnp.repeat(jnp.exp(heights), shape[position] // shards_of).reshape((-1,) + (1,) * (len(shape) - 1 - position))
    return gain


def gaussian(rng, dims, deviation, limit, cuts=(), dtype=jnp.bfloat16):
    values = jax.random.normal(rng, dims, jnp.float32) * deviation
    if len(cuts) > 0:
        values = steps_of(rng, dims, cuts, -0.22, 0.18) * values
    return jnp.clip(values, min=-limit, max=limit).astype(dtype)


def setup_inputs(seed: int = 0) -> dict:
    seeds = jax.random.split(jax.random.key(seed), 6)
    tokens = gaussian(seeds[0], (TOKENS, D), 1.0, 6.0, ((0, 16), (1, 16)))
    ln_gain = jnp.clip(1.0 + 0.18 * jax.random.normal(seeds[1], (D,), jnp.float32), 0.1, 1.9)
    projected = draw_projected(jax.random.fold_in(seeds[5], 71), 0)
    out_grad = gaussian(seeds[3], (TOKENS, HH), 4.0, 24.0, ((0, 16), (1, 16)))
    w_joined = gaussian(seeds[4], (D, 3, HH), D ** -0.5, 0.078125, ((2, 16),))
    return {"tokens": tokens, "ln_gain": ln_gain, "projected": projected, "out_grad": out_grad, "w_joined": w_joined}


def product(form, left, right):
    return jnp.einsum(form, left.astype(jnp.float32), right.astype(jnp.float32), precision=lax.Precision.HIGHEST)

def attention_grad(projected, out_grad):
    queries = projected[:, :, 0]
    keys_all = projected[:, :, 1]
    values = projected[:, :, 2]
    scaling = projected.shape[-1] ** (-0.5)
    scores = product('bqhd,bkhd->bhqk', queries, keys_all) * scaling
    raised = jnp.exp(scores - lax.optimization_barrier(jnp.max(scores, axis=-1, keepdims=True)))
    attn_probs = raised / lax.optimization_barrier(jnp.sum(raised, axis=-1, keepdims=True))
    probs_low = attn_probs.astype(jnp.bfloat16)
    value_grad = product('bhqk,bqhd->bkhd', probs_low, out_grad)
    prob_grad = product('bqhd,bkhd->bhqk', out_grad, values)
    score_grad = attn_probs * (prob_grad - lax.optimization_barrier(jnp.sum(attn_probs * prob_grad, axis=-1, keepdims=True)))
    score_low = score_grad.astype(jnp.bfloat16)
    query_grad = product('bhqk,bkhd->bqhd', score_low, keys_all) * scaling
    key_grad = product('bhqk,bqhd->bkhd', score_low, queries) * scaling
    return jnp.stack([query_grad, key_grad, value_grad], axis=2).astype(jnp.bfloat16)

def normalize(tokens):
    values = tokens.astype(jnp.float32)
    center = lax.optimization_barrier(jnp.mean(values, axis=-1, keepdims=True))
    spread = lax.optimization_barrier(jnp.mean(jnp.square(values - center), axis=-1, keepdims=True))
    inverse = lax.rsqrt(spread + 1e-06)
    return ((values - center) * inverse, inverse)

def image_grad(operand):
    return attention_grad(operand[0], operand[1])

def reference(tokens, ln_gain, projected, out_grad, w_joined):
    x_hat, inverse = normalize(tokens)
    normed = (x_hat * ln_gain).astype(jnp.bfloat16)
    images = TOKENS // SEQ
    proj_images = projected.reshape(images, 1, SEQ, 3, HEADS, HDIM)
    grad_images = out_grad.reshape(images, 1, SEQ, HEADS, HDIM)
    grad_proj = lax.map(image_grad, (proj_images, grad_images))
    grad_flat = grad_proj.reshape(TOKENS, 3 * HEADS * HDIM)
    grad_weight = jnp.dot(normed.T, grad_flat, preferred_element_type=jnp.float32).reshape(D, 3, HEADS * HDIM)
    w_flat = w_joined.reshape(D, 3 * HEADS * HDIM)
    grad_normed = jnp.dot(grad_flat, w_flat.T, preferred_element_type=jnp.float32)
    scaled = grad_normed * ln_gain
    mean_plain = lax.optimization_barrier(jnp.mean(scaled, axis=-1, keepdims=True))
    mean_hat = lax.optimization_barrier(jnp.mean(scaled * x_hat, axis=-1, keepdims=True))
    grad_input = ((scaled - mean_plain - x_hat * mean_hat) * inverse).astype(jnp.bfloat16)
    return (grad_weight, grad_input)
```

```python
import functools

import jax
import jax.numpy as jnp
from jax import lax
from jax.experimental import pallas as pl
from jax.experimental.pallas import tpu as pltpu
from jax.sharding import PartitionSpec as P

MESH = pl.DeviceIdType.MESH
F32 = jnp.float32
BF16 = jnp.bfloat16

D = 6144
HDIM = 128
SEQ = 512
COLS = 384
WIDTH = 256
HALF = SEQ // 2
GROWS = 3 * WIDTH
GHALF = GROWS // 2
SCALE = HDIM ** (-0.5)
LANES = 128

NT = (((1,), (1,)), ((), ()))
NN = (((1,), (0,)), ((), ()))
TN = (((0,), (0,)), ((), ()))


def slot(dz, dx):
    m = 7 if abs(dz) == 4 else (2 * abs(dz) - (1 if dz < 0 else 0))
    return dx * 8 + m


GATHER = [
    ("z+", (0, 0), None), ("z-", (0, 0), None), ("x", (0, 0), None),
    ("z+", (-1, 0), None), ("z-", (1, 0), None), ("x", (-1, 0), None),
    ("z+", (-2, 0), None), ("z-", (2, 0), None), ("x", (-2, 0), None),
    ("z+", (-3, 0), 0), ("z-", (3, 0), 1), ("x", (2, 0), None),
    ("z+", (-2, 1), None), ("x", (1, 0), None),
    ("z-", (2, 1), None), ("z+", (-3, 1), 0), ("z-", (3, 1), 1),
]


def dot(left, right, dims):
    return lax.dot_general(left, right, dims, preferred_element_type=F32)


def add_into(dst, sources, rows, chunk=64):
    def body(i, carry):
        at = pl.ds(pl.multiple_of(i * chunk, chunk), chunk)
        total = dst[at, :].astype(F32)
        for source in sources:
            total = total + source[at, :].astype(F32)
        dst[at, :] = total.astype(BF16)
        return carry

    lax.fori_loop(0, rows // chunk, body, 0)


def pack_rows(acc, out, first):
    for i in range(4):
        part = acc[i * LANES : (i + 1) * LANES, :]
        out[first + i : first + i + 1, :] = jnp.sum(part.T, axis=0, keepdims=True)


def spread_rows(rows, out):
    for i in range(4):
        out[i * LANES : (i + 1) * LANES, :] = jnp.broadcast_to(rows[i : i + 1, :], (LANES, LANES)).T


def kernel(
    tok, gain, proj, og, w, gw_out, gi_out,
    ag, wv, pv, ov, gp, gpt, part, halves, landed, gsum, cland, yland, yhalf, xland, normed,
    acc_a, acc_b, mean_b, inv_b, st_send, st_recv, sz_send, sz_recv,
    load_sem, ag_s, ag_r, st_s, st_r, sz_s, sz_r, rs_s, rs_r, c_s, c_r, y_s, y_r,
):
    dp, mp = lax.axis_index("dp"), lax.axis_index("mp")
    y, xh, c = dp // 4, (dp // 2) % 2, dp % 2
    z, x = mp // 2, mp % 2

    def at_z(k):
        return (dp, ((z + k + 8) % 8) * 2 + x)

    at_x = (dp, z * 2 + 1 - x)
    at_c = (y * 4 + xh * 2 + 1 - c, mp)
    at_xh = (y * 4 + (1 - xh) * 2 + c, mp)

    def at_y(k):
        return (((y + k + 4) % 4) * 4 + xh * 2 + c, mp)

    def remote(src, dst, send, recv, device):
        return pltpu.make_async_remote_copy(
            src_ref=src, dst_ref=dst, send_sem=send, recv_sem=recv, device_id=device, device_id_type=MESH
        )

    loads = [
        pltpu.make_async_copy(tok, ag.at[0], load_sem.at[0]),
        pltpu.make_async_copy(proj, pv, load_sem.at[1]),
        pltpu.make_async_copy(og, ov, load_sem.at[2]),
        pltpu.make_async_copy(w, wv, load_sem.at[3]),
    ]
    for load in loads:
        load.start()

    barrier = pltpu.get_barrier_semaphore()
    peers = [at_z(k) for k in range(1, 8)] + [at_x, at_c, at_xh, at_y(1), at_y(-1)]
    for peer in peers:
        pl.semaphore_signal(barrier, inc=1, device_id=peer, device_id_type=MESH)
    pl.semaphore_wait(barrier, len(peers))

    def gather(e):
        channel, (dz, dx), half = GATHER[e]
        if channel == "x":
            there, device = slot(dz, 1 - dx), at_x
        else:
            step = 1 if channel == "z+" else -1
            there, device = slot(dz - step, dx), at_z(step)
        here = slot(dz, dx)
        if half is None:
            src = tok if here == 0 else ag.at[here]
            dst = ag.at[there]
        else:
            src = ag.at[here, pl.ds(half * HALF, HALF)]
            dst = ag.at[there, pl.ds(half * HALF, HALF)]
        return remote(src, dst, ag_s.at[e], ag_r.at[e], device)

    for e in (0, 1, 2):
        gather(e).start()

    def exchange_x(n):
        return remote(st_send.at[n], st_recv.at[n], st_s.at[n], st_r.at[n], at_x)

    def exchange_z(n, k):
        return remote(sz_send.at[n], sz_recv.at[n, k], sz_s.at[n, k], sz_r.at[n, k], at_z(k))

    loads[0].wait()
    for i in range(4):
        rows = slice(i * LANES, (i + 1) * LANES)
        tiles = [ag[0, rows, k * LANES : (k + 1) * LANES].astype(F32) for k in range(3)]
        sums = tiles[0] + tiles[1] + tiles[2]
        center = jnp.sum(sums, axis=1, keepdims=True) / COLS
        acc_a[rows, :] = sums
        acc_b[rows, :] = sum(jnp.square(tile - center) for tile in tiles)
    pack_rows(acc_a, st_send.at[0], 0)
    pack_rows(acc_b, st_send.at[0], 4)
    st_send[0, 0:4, :] = st_send[0, 0:4, :] / COLS
    exchange_x(0).start()

    def head(h):
        cols = slice(h * HDIM, (h + 1) * HDIM)
        queries, keys_all, values, upstream = pv[0, :, cols], pv[1, :, cols], pv[2, :, cols], ov[:, cols]
        key_grad = value_grad = None
        for q0 in range(0, SEQ, 256):
            qs = slice(q0, q0 + 256)
            scores = dot(keys_all, queries[qs], NT) * SCALE
            raised = jnp.exp(scores - jnp.max(scores, axis=0, keepdims=True))
            probs = raised / jnp.sum(raised, axis=0, keepdims=True)
            term = dot(probs.astype(BF16), upstream[qs], NN)
            value_grad = term if value_grad is None else value_grad + term
            prob_grad = dot(values, upstream[qs], NT)
            score_grad = probs * (prob_grad - jnp.sum(probs * prob_grad, axis=0, keepdims=True))
            score_low = score_grad.astype(BF16)
            term = dot(score_low, queries[qs], NN)
            key_grad = term if key_grad is None else key_grad + term
            gp[0, qs, cols] = (dot(score_low, keys_all, TN) * SCALE).astype(BF16)
        gp[1, :, cols] = (key_grad * SCALE).astype(BF16)
        gp[2, :, cols] = value_grad.astype(BF16)

    loads[1].wait()
    loads[2].wait()
    head(0)

    exchange_x(0).wait_recv()
    mine, other = st_send[0], st_recv[0]
    center = (mine[0:4] + other[0:4]) * 0.5
    sz_send[0, 0:4, :] = center
    sz_send[0, 4:8, :] = mine[4:8] + other[4:8] + COLS * (
        jnp.square(mine[0:4] - center) + jnp.square(other[0:4] - center)
    )
    for k in range(1, 8):
        exchange_z(0, k).start()

    gather(0).wait_recv()
    gather(3).start()
    gather(1).wait_recv()
    gather(4).start()
    gather(2).wait_recv()
    gather(5).start()

    head(1)
    for k in range(3):
        gpt[k] = gp[k].T

    gather(3).wait_recv()
    gather(6).start()
    gather(4).wait_recv()
    gather(7).start()
    gather(5).wait_recv()
    gather(8).start()

    for k in range(1, 8):
        exchange_z(0, k).wait_recv()
    centers = [sz_send[0, 0:4, :]] + [sz_recv[0, k, 0:4, :] for k in range(1, 8)]
    squares = [sz_send[0, 4:8, :]] + [sz_recv[0, k, 4:8, :] for k in range(1, 8)]
    center = sum(centers) * 0.125
    spread = (sum(squares) + (2 * COLS) * sum(jnp.square(one - center) for one in centers)) / D
    spread_rows(center, mean_b)
    spread_rows(lax.rsqrt(spread + 1e-06), inv_b)

    def owner(n):
        m = n % 8
        dz = ((m + 1) // 2) * (1 - 2 * (m % 2))
        return ((z + dz + 8) % 8) * 2 + (x + n // 8) % 2

    loads[3].wait()

    def share(n, carry):
        first = pl.multiple_of(owner(n) * COLS, COLS)
        total = dot(gp[0], wv[0, pl.ds(first, COLS), :], NT)
        total = total + dot(gp[1], wv[1, pl.ds(first, COLS), :], NT)
        total = total + dot(gp[2], wv[2, pl.ds(first, COLS), :], NT)
        part[n] = total.astype(BF16)
        return carry

    lax.fori_loop(0, 16, share, 0)

    gather(6).wait_recv()
    gather(9).start()
    gather(7).wait_recv()
    gather(10).start()
    gather(8).wait_recv()
    gather(12).start()
    gather(11).start()

    acc_a[...] = jnp.zeros_like(acc_a)
    acc_b[...] = jnp.zeros_like(acc_b)

    def reduce_half(sign, dx):
        n = (0 if sign > 0 else 1) + 2 * dx
        half = 1 if sign > 0 else 0
        src = part.at[slot(4, dx), pl.ds(half * HALF, HALF)]
        return remote(src, halves.at[n], rs_s.at[13 + n], rs_r.at[13 + n], at_z(sign))

    def reduce_z(sign, k, dx):
        n = {(3, 1): 0, (3, 0): 2, (2, 0): 4, (1, 0): 6}[(k, dx)] + (0 if sign > 0 else 1)
        return remote(part.at[slot(sign * k, dx)], landed.at[n], rs_s.at[n], rs_r.at[n], at_z(sign))

    def reduce_x(dz):
        n = {1: 8, -1: 9, 2: 10, -2: 11, 0: 12}[dz]
        return remote(part.at[slot(dz, 1)], landed.at[n], rs_s.at[n], rs_r.at[n], at_x)

    def block_index(dy, dxh, dc):
        return ((y + dy) % 4) * 4 + ((xh + dxh) % 2) * 2 + (c + dc) % 2

    def core_copy(j, k):
        return remote(gsum.at[j], cland.at[k], c_s.at[k], c_r.at[k], at_c)

    def weight(i, carry):
        q = i % 8
        cross = q + (q + 6) // 8 - 4 * ((q + 3) // 8) + 3 * ((q + 2) // 8)
        n = i + (i // 8) * (cross - q)

        @pl.when(i == 7)
        def _():
            gather(9).wait_recv()
            gather(10).wait_recv()

        @pl.when(i == 8)
        def _():
            gather(11).wait_recv()
            gather(14).start()
            gather(13).start()

        @pl.when(i == 12)
        def _():
            gather(12).wait_recv()
            gather(15).start()

        @pl.when(i == 13)
        def _():
            gather(14).wait_recv()
            gather(16).start()
            gather(13).wait_recv()
            reduce_x(1).start()

        @pl.when(i == 15)
        def _():
            gather(15).wait_recv()
            gather(16).wait_recv()
            reduce_half(1, 1).start()
            reduce_half(-1, 1).start()

        j = owner(n)

        def rows_step(r, carry):
            rows = pl.ds(pl.multiple_of(r * 64, 64), 64)
            center, inverse = mean_b[rows, :], inv_b[rows, :]
            plain, hat = acc_a[rows, :], acc_b[rows, :]
            for k in range(3):
                lanes = slice(k * LANES, (k + 1) * LANES)
                scale = gain[j, :, lanes]
                value = (ag[n, rows, lanes].astype(F32) - center) * inverse * scale
                normed[rows, lanes] = value.astype(BF16)
                piece = part[n, rows, lanes].astype(F32)
                plain = plain + piece * scale
                hat = hat + piece * value
            acc_a[rows, :] = plain
            acc_b[rows, :] = hat
            return carry

        lax.fori_loop(0, SEQ // 64, rows_step, 0)
        for k in range(3):
            gsum[j, k * WIDTH : (k + 1) * WIDTH, :] = dot(gpt[k], normed[...], NN).astype(BF16)

        @pl.when((j + c) % 2 == 1)
        def _():
            core_copy(j, ((j // 4 - y + 4) % 4) * 2 + (j // 2 + xh) % 2).start()

        return carry

    lax.fori_loop(0, 16, weight, 0)

    pack_rows(acc_a, st_send.at[1], 0)
    pack_rows(acc_b, st_send.at[1], 4)
    exchange_x(1).start()

    def core_add(dy, dxh):
        k = dy * 2 + dxh
        core_copy(0, k).wait_recv()
        add_into(cland.at[k], [gsum.at[block_index(dy, dxh, 0)]], GROWS)

    def y_half(sign, dxh):
        n = dxh * 2 + (0 if sign > 0 else 1)
        half = 0 if sign > 0 else 1
        src = cland.at[4 + dxh, pl.ds(half * GHALF, GHALF)]
        return remote(src, yhalf.at[n], y_s.at[n], y_r.at[n], at_y(sign))

    def y_full(sign, dxh):
        n = dxh * 2 + (0 if sign > 0 else 1)
        src = cland.at[(2 if sign > 0 else 6) + dxh]
        return remote(src, yland.at[n], y_s.at[4 + n], y_r.at[4 + n], at_y(sign))

    def y_pass(dxh):
        for sign, dy, half in ((1, 1, 0), (-1, 3, 1)):
            n = dxh * 2 + (0 if sign > 0 else 1)
            y_half(sign, dxh).wait_recv()
            add_into(cland.at[dy * 2 + dxh, pl.ds(half * GHALF, GHALF)], [yhalf.at[n]], GHALF)
            y_full(sign, dxh).start()

    x_copy = remote(cland.at[1], xland, y_s.at[8], y_r.at[8], at_xh)

    core_add(2, 1)
    y_half(1, 1).start()
    y_half(-1, 1).start()
    core_add(1, 1)
    core_add(3, 1)

    for sign, n in ((1, 2), (-1, 3)):
        reduce_half(sign, 1).wait_recv()
        half = 1 if sign > 0 else 0
        add_into(part.at[slot(3 * sign, 1), pl.ds(half * HALF, HALF)], [halves.at[n]], HALF)
        reduce_z(sign, 3, 1).start()
    reduce_x(-1).start()

    exchange_x(1).wait_recv()
    sz_send[1] = st_send[1] + st_recv[1]
    for k in range(1, 8):
        exchange_z(1, k).start()

    y_pass(1)
    core_add(2, 0)
    core_add(0, 1)
    core_add(1, 0)
    core_add(3, 0)
    core_add(0, 0)

    for sign, n in ((1, 0), (-1, 1)):
        reduce_z(sign, 3, 1).wait_recv()
        add_into(part.at[slot(2 * sign, 1)], [landed.at[n]], SEQ)
        reduce_x(2 * sign).start()
        reduce_half(sign, 0).start()

    for k in range(1, 8):
        exchange_z(1, k).wait_recv()
    sums = (sz_send[1] + sum(sz_recv[1, k] for k in range(1, 8))) / D
    spread_rows(sums[0:4], acc_a)
    spread_rows(sums[4:8], acc_b)

    for sign, n in ((1, 0), (-1, 1)):
        reduce_half(sign, 0).wait_recv()
        half = 1 if sign > 0 else 0
        add_into(part.at[slot(3 * sign, 0), pl.ds(half * HALF, HALF)], [halves.at[n]], HALF)
        reduce_z(sign, 3, 0).start()

    y_full(1, 1).wait_recv()
    y_full(-1, 1).wait_recv()
    y_half(1, 0).start()
    y_half(-1, 0).start()
    add_into(cland.at[1], [yland.at[2], yland.at[3]], GROWS)
    x_copy.start()

    for sign, n in ((1, 0), (-1, 1)):
        reduce_z(sign, 3, 0).wait_recv()
        reduce_x(2 * sign).wait_recv()
        add_into(part.at[slot(2 * sign, 0)], [landed.at[2 + n], landed.at[10 + n]], SEQ)
        reduce_z(sign, 2, 0).start()
    reduce_x(0).start()

    y_pass(0)

    for sign, n in ((1, 0), (-1, 1)):
        reduce_z(sign, 2, 0).wait_recv()
        reduce_x(sign).wait_recv()
        add_into(part.at[slot(sign, 0)], [landed.at[4 + n], landed.at[8 + n]], SEQ)
        reduce_z(sign, 1, 0).start()

    y_full(1, 0).wait_recv()
    y_full(-1, 0).wait_recv()
    x_copy.wait_recv()
    for k in range(3):

        def out_step(r, carry, k=k):
            rows = pl.ds(pl.multiple_of(k * WIDTH + r * LANES, LANES), LANES)
            total = cland[0, rows, :].astype(F32) + xland[rows, :].astype(F32)
            total = total + yland[0, rows, :].astype(F32) + yland[1, rows, :].astype(F32)
            gw_out[k, :, pl.ds(pl.multiple_of(r * LANES, LANES), LANES)] = total.T
            return carry

        lax.fori_loop(0, WIDTH // LANES, out_step, 0)

    reduce_z(1, 1, 0).wait_recv()
    reduce_z(-1, 1, 0).wait_recv()
    reduce_x(0).wait_recv()

    def in_step(r, carry):
        rows = pl.ds(pl.multiple_of(r * 64, 64), 64)
        center, inverse = mean_b[rows, :], inv_b[rows, :]
        plain, hat = acc_a[rows, :], acc_b[rows, :]
        for k in range(3):
            lanes = slice(k * LANES, (k + 1) * LANES)
            total = part[0, rows, lanes].astype(F32) + landed[6, rows, lanes].astype(F32)
            total = total + landed[7, rows, lanes].astype(F32) + landed[12, rows, lanes].astype(F32)
            x_hat = (ag[0, rows, lanes].astype(F32) - center) * inverse
            scaled = total * gain[mp, :, lanes]
            gi_out[rows, lanes] = ((scaled - plain - x_hat * hat) * inverse).astype(BF16)
        return carry

    lax.fori_loop(0, SEQ // 64, in_step, 0)

    for e in range(len(GATHER)):
        gather(e).wait_send()
    for n in range(2):
        exchange_x(n).wait_send()
        for k in range(1, 8):
            exchange_z(n, k).wait_send()
    for k in range(8):
        core_copy(0, k).wait_send()
    x_copy.wait_send()
    for dz in (1, -1, 2, -2, 0):
        reduce_x(dz).wait_send()
    for sign in (1, -1):
        for n in (0, 1):
            reduce_half(sign, n).wait_send()
            y_half(sign, n).wait_send()
            y_full(sign, n).wait_send()
        for k, dx in ((3, 1), (3, 0), (2, 0), (1, 0)):
            reduce_z(sign, k, dx).wait_send()


def shards(tokens, ln_gain, projected, out_grad, w_joined):
    vmem = pltpu.VMEM
    dma = pltpu.SemaphoreType.DMA
    hbm = pl.BlockSpec(memory_space=pl.ANY)
    local = pl.BlockSpec(memory_space=pltpu.VMEM)
    grad_weight, grad_input = pl.pallas_call(
        kernel,
        out_shape=(
            jax.ShapeDtypeStruct((3, COLS, WIDTH), F32),
            jax.ShapeDtypeStruct((SEQ, COLS), BF16),
        ),
        in_specs=[hbm, local, hbm, hbm, hbm],
        out_specs=(local, local),
        scratch_shapes=[
            vmem((16, SEQ, COLS), BF16),
            vmem((3, D, WIDTH), BF16),
            vmem((3, SEQ, WIDTH), BF16),
            vmem((SEQ, WIDTH), BF16),
            vmem((3, SEQ, WIDTH), BF16),
            vmem((3, WIDTH, SEQ), BF16),
            vmem((16, SEQ, COLS), BF16),
            vmem((4, HALF, COLS), BF16),
            vmem((13, SEQ, COLS), BF16),
            vmem((16, GROWS, COLS), BF16),
            vmem((8, GROWS, COLS), BF16),
            vmem((4, GROWS, COLS), BF16),
            vmem((4, GHALF, COLS), BF16),
            vmem((GROWS, COLS), BF16),
            vmem((SEQ, COLS), BF16),
            vmem((SEQ, LANES), F32),
            vmem((SEQ, LANES), F32),
            vmem((SEQ, LANES), F32),
            vmem((SEQ, LANES), F32),
            vmem((2, 8, LANES), F32),
            vmem((2, 8, LANES), F32),
            vmem((2, 8, LANES), F32),
            vmem((2, 8, 8, LANES), F32),
            dma((4,)),
            dma((17,)), dma((17,)),
            dma((2,)), dma((2,)),
            dma((2, 8)), dma((2, 8)),
            dma((17,)), dma((17,)),
            dma((8,)), dma((8,)),
            dma((9,)), dma((9,)),
        ],
        compiler_params=pltpu.CompilerParams(
            collective_id=0, has_side_effects=True, vmem_limit_bytes=62 * 1024 * 1024
        ),
        cost_estimate=pl.CostEstimate(flops=11_000_000_000, bytes_accessed=14_000_000, transcendentals=600_000),
        name="parallel_block_backward",
    )(
        tokens,
        ln_gain.reshape(16, 1, COLS),
        jnp.transpose(projected, (1, 0, 2)),
        out_grad,
        jnp.transpose(w_joined, (1, 0, 2)),
    )
    return jnp.transpose(grad_weight, (1, 0, 2)), grad_input


def solution(mesh):
    in_specs = (P("dp", "mp"), P(), P("dp", None, "mp"), P("dp", "mp"), P(None, None, "mp"))
    out_specs = (P("dp", None, "mp"), P("dp", "mp"))
    return jax.shard_map(shards, mesh=mesh, in_specs=in_specs, out_specs=out_specs, check_vma=False)
```

```python
import functools

import jax
import jax.numpy as jnp
from jax import lax
from jax.experimental import pallas as pl
from jax.experimental.pallas import tpu as pltpu
from jax.sharding import PartitionSpec as P

MESH = pl.DeviceIdType.MESH
F32 = jnp.float32
BF16 = jnp.bfloat16

D = 6144
HDIM = 128
SEQ = 512
COLS = 384
WIDTH = 256
HALF = SEQ // 2
GCOLS = 3 * HDIM
GHALF = GCOLS // 2
SCALE = HDIM ** (-0.5)
LANES = 128

NT = (((1,), (1,)), ((), ()))
NN = (((1,), (0,)), ((), ()))
TN = (((0,), (0,)), ((), ()))


def slot(dz):
    return 7 if abs(dz) == 4 else (2 * abs(dz) - (1 if dz < 0 else 0))


def dot(left, right, dims):
    return lax.dot_general(left, right, dims, preferred_element_type=F32)


def add_into(dst, sources, rows, chunk=64):
    def body(i, carry):
        at = pl.ds(pl.multiple_of(i * chunk, chunk), chunk)
        total = dst[at, :].astype(F32)
        for source in sources:
            total = total + source[at, :].astype(F32)
        dst[at, :] = total.astype(BF16)
        return carry

    lax.fori_loop(0, rows // chunk, body, 0)


def pack_rows(acc, out, first):
    for i in range(4):
        part = acc[i * LANES : (i + 1) * LANES, :]
        out[first + i : first + i + 1, :] = jnp.sum(part.T, axis=0, keepdims=True)


def spread_rows(rows, out):
    for i in range(4):
        out[i * LANES : (i + 1) * LANES, :] = jnp.broadcast_to(rows[i : i + 1, :], (LANES, LANES)).T


def kernel(
    tok, gain, proj, og, w, gw_out, gi_out,
    ag, wv, wx, pv, ov, gp, gpt, norm, part, rland, gsum, cland, yland, yhalf, xland, fin, last,
    acc_a, acc_b, mean_b, inv_b, st_send, st_recv, sz_send, sz_recv,
    load_sem, w_sem, ag_s, ag_r, st_s, st_r, sz_s, sz_r, wx_s, wx_r, wc_s, wc_r, gp_s, gp_r,
    rs_s, rs_r, c_s, c_r, y_s, y_r, x_s, x_r, f_s, f_r,
):
    dp, mp = lax.axis_index("dp"), lax.axis_index("mp")
    y, xh, c = dp // 4, (dp // 2) % 2, dp % 2
    z, x = mp // 2, mp % 2

    def at_z(k):
        return (dp, ((z + k + 8) % 8) * 2 + x)

    def at_y(k):
        return (((y + k + 4) % 4) * 4 + xh * 2 + c, mp)

    sibling = y * 4 + xh * 2 + 1 - c
    at_c = (sibling, mp)
    at_x = (dp, z * 2 + 1 - x)
    at_xc = (sibling, z * 2 + 1 - x)
    at_xh = (y * 4 + (1 - xh) * 2 + c, mp)
    at_xo = (y * 4 + (1 - xh) * 2 + c, z * 2 + 1 - x)

    def remote(src, dst, send, recv, device):
        return pltpu.make_async_remote_copy(
            src_ref=src, dst_ref=dst, send_sem=send, recv_sem=recv, device_id=device, device_id_type=MESH
        )

    def zed(n):
        return (z + ((n + 1) // 2) * (1 - 2 * (n % 2)) + 8) % 8

    def w_rows(n, column):
        return w.at[:, pl.ds(pl.multiple_of((zed(n) * 2 + column) * COLS, COLS), COLS), :]

    loads = [
        pltpu.make_async_copy(tok, ag.at[0], load_sem.at[0]),
        pltpu.make_async_copy(proj, pv, load_sem.at[1]),
        pltpu.make_async_copy(og, ov, load_sem.at[2]),
    ]
    for load in loads:
        load.start()

    def w_load(n):
        return pltpu.make_async_copy(w_rows(n, x), wv.at[n], w_sem.at[n])

    barrier = pltpu.get_barrier_semaphore()
    peers = [at_z(k) for k in range(1, 8)] + [at_c, at_x, at_xc, at_xh, at_xo, at_y(1), at_y(-1)]
    for peer in peers:
        pl.semaphore_signal(barrier, inc=1, device_id=peer, device_id_type=MESH)
    pl.semaphore_wait(barrier, len(peers))

    def gather(sign, k):
        hop = (k - 1) // 2
        half = (0 if sign > 0 else 1) if k % 2 == 1 else (1 if sign > 0 else 0)
        rows = pl.ds(half * HALF, HALF)
        src = tok.at[rows] if hop == 0 else ag.at[slot(-sign * hop), rows]
        e = (0 if sign > 0 else 7) + k - 1
        return remote(src, ag.at[slot(-sign * (hop + 1)), rows], ag_s.at[e], ag_r.at[e], at_z(sign))

    def gather_event(k):
        for sign in (1, -1):
            gather(sign, k).wait_recv()
            if k <= 5:
                gather(sign, k + 2).start()

    for k in (1, 2):
        gather(1, k).start()
        gather(-1, k).start()

    def w_place(d, core):
        return 2 * ((y - d + 4) % 4) + 1 - core

    def w_cross():
        n = w_place(0, c)
        partner = (y * 4 + ((xh + c) % 2) * 2 + c, z * 2 + 1 - x)
        return remote(w_rows(n, 1 - x), wx.at[n], wx_s.at[0], wx_r.at[0], partner)

    def w_ring(sign):
        n = w_place(0, c)
        e = 1 if sign > 0 else 2
        return remote(wx.at[n], wx.at[n], wx_s.at[e], wx_r.at[e], at_y(sign))

    def w_ring_far(sign):
        n = w_place(sign, c)
        e = 3 if sign > 0 else 4
        rows = pl.ds(0 if sign > 0 else COLS // 2, COLS // 2)
        return remote(wx.at[n, :, rows], wx.at[n, :, rows], wx_s.at[e], wx_r.at[e], at_y(sign))

    def w_core(i):
        n = w_place((0, 1, -1, 2)[i], c)
        return remote(wx.at[n], wx.at[n], wc_s.at[i], wc_r.at[i], at_c)

    w_cross().start()
    for n in (7, 6, 5, 4, 3, 2, 1, 0):
        w_load(n).start()

    def exchange_x(n):
        return remote(st_send.at[n], st_recv.at[n], st_s.at[n], st_r.at[n], at_x)

    def exchange_z(n, k):
        return remote(sz_send.at[n], sz_recv.at[n, k], sz_s.at[n, k], sz_r.at[n, k], at_z(k))

    loads[0].wait()
    for i in range(4):
        rows = slice(i * LANES, (i + 1) * LANES)
        tiles = [ag[0, rows, k * LANES : (k + 1) * LANES].astype(F32) for k in range(3)]
        sums = tiles[0] + tiles[1] + tiles[2]
        center = jnp.sum(sums, axis=1, keepdims=True) / COLS
        acc_a[rows, :] = sums
        acc_b[rows, :] = sum(jnp.square(tile - center) for tile in tiles)
    pack_rows(acc_a, st_send.at[0], 0)
    pack_rows(acc_b, st_send.at[0], 4)
    st_send[0, 0:4, :] = st_send[0, 0:4, :] / COLS
    exchange_x(0).start()

    def gp_copy(h):
        lanes = pl.ds(h * HDIM, HDIM)
        return remote(gp.at[0, :, :, lanes], gp.at[1, :, :, lanes], gp_s.at[h], gp_r.at[h], at_x)

    def head(h):
        cols = slice(h * HDIM, (h + 1) * HDIM)
        queries, keys_all, values, upstream = pv[0, :, cols], pv[1, :, cols], pv[2, :, cols], ov[:, cols]
        key_grad = value_grad = None
        for q0 in range(0, SEQ, 256):
            qs = slice(q0, q0 + 256)
            scores = dot(keys_all, queries[qs], NT) * SCALE
            raised = jnp.exp(scores - jnp.max(scores, axis=0, keepdims=True))
            probs = raised / jnp.sum(raised, axis=0, keepdims=True)
            term = dot(probs.astype(BF16), upstream[qs], NN)
            value_grad = term if value_grad is None else value_grad + term
            prob_grad = dot(values, upstream[qs], NT)
            score_grad = probs * (prob_grad - jnp.sum(probs * prob_grad, axis=0, keepdims=True))
            score_low = score_grad.astype(BF16)
            term = dot(score_low, queries[qs], NN)
            key_grad = term if key_grad is None else key_grad + term
            gp[0, 0, qs, cols] = (dot(score_low, keys_all, TN) * SCALE).astype(BF16)
        gp[0, 1, :, cols] = (key_grad * SCALE).astype(BF16)
        gp[0, 2, :, cols] = value_grad.astype(BF16)
        gp_copy(h).start()

    def turn(s, h):
        for k in range(3):
            gpt[s, h, k * HDIM : (k + 1) * HDIM, :] = gp[s, k, :, h * HDIM : (h + 1) * HDIM].T

    loads[1].wait()
    loads[2].wait()
    head(0)

    exchange_x(0).wait_recv()
    mine, other = st_send[0], st_recv[0]
    center = (mine[0:4] + other[0:4]) * 0.5
    sz_send[0, 0:4, :] = center
    sz_send[0, 4:8, :] = mine[4:8] + other[4:8] + COLS * (
        jnp.square(mine[0:4] - center) + jnp.square(other[0:4] - center)
    )
    for k in range(1, 8):
        exchange_z(0, k).start()

    gather_event(1)
    w_cross().wait_recv()
    w_ring(1).start()
    w_ring(-1).start()
    w_core(0).start()
    gather_event(2)

    head(1)

    gather_event(3)
    turn(0, 0)
    turn(0, 1)

    for k in range(1, 8):
        exchange_z(0, k).wait_recv()
    centers = [sz_send[0, 0:4, :]] + [sz_recv[0, k, 0:4, :] for k in range(1, 8)]
    squares = [sz_send[0, 4:8, :]] + [sz_recv[0, k, 4:8, :] for k in range(1, 8)]
    center = sum(centers) * 0.125
    spread = (sum(squares) + (2 * COLS) * sum(jnp.square(one - center) for one in centers)) / D
    spread_rows(center, mean_b)
    spread_rows(lax.rsqrt(spread + 1e-06), inv_b)
    gather_event(4)

    acc_a[...] = jnp.zeros_like(acc_a)
    acc_b[...] = jnp.zeros_like(acc_b)

    def core_copy(s, o):
        return remote(gsum.at[s, o, 1 - c], cland.at[s, o], c_s.at[s, o], c_r.at[s, o], at_c)

    def weight(s, n):
        o = ((zed(n) // 2 - y + 4) % 4) * 2 + (zed(n) + xh) % 2
        for h in range(2):
            gsum[s, o, h] = dot(gpt[s, h], norm[n], NN).astype(BF16)
        core_copy(s, o).start()

    def weight_own(n, carry):
        j = zed(n) * 2 + x

        def rows_step(r, carry):
            rows = pl.ds(pl.multiple_of(r * 64, 64), 64)
            center, inverse = mean_b[rows, :], inv_b[rows, :]
            for k in range(3):
                lanes = slice(k * LANES, (k + 1) * LANES)
                value = (ag[n, rows, lanes].astype(F32) - center) * inverse * gain[j, :, lanes]
                norm[n, rows, lanes] = value.astype(BF16)
            return carry

        lax.fori_loop(0, SEQ // 64, rows_step, 0)
        weight(0, n)
        return carry

    def weight_cross(n, carry):
        weight(1, n)
        return carry

    def share(n):
        for k in range(3):
            term = dot(gp[0, k], wv[n, k], NT) + dot(gp[1, k], wx[n, k], NT)
            total = term if k == 0 else total + term
        part[n] = total.astype(BF16)

    def sums(n):
        j = zed(n) * 2 + x

        def rows_step(r, carry):
            rows = pl.ds(pl.multiple_of(r * 64, 64), 64)
            plain, hat = acc_a[rows, :], acc_b[rows, :]
            for k in range(3):
                lanes = slice(k * LANES, (k + 1) * LANES)
                piece = part[n, rows, lanes].astype(F32)
                plain = plain + piece * gain[j, :, lanes]
                hat = hat + piece * norm[n, rows, lanes].astype(F32)
            acc_a[rows, :] = plain
            acc_b[rows, :] = hat
            return carry

        lax.fori_loop(0, SEQ // 64, rows_step, 0)

    def share_far(i, carry):
        share(7 - i)
        return carry

    def share_near(i, carry):
        share(4 - i)
        sums(4 - i)
        return carry

    def sums_far(i, carry):
        sums(7 - i)
        return carry

    def reduce(sign, k):
        dz = sign * (4 - k // 2)
        first = 1 if sign > 0 else 0
        half = first if k % 2 == 1 else 1 - first
        e = (0 if sign > 0 else 7) + k - 1
        return remote(
            part.at[slot(dz), pl.ds(half * HALF, HALF)], rland.at[e], rs_s.at[e], rs_r.at[e], at_z(sign)
        )

    def reduce_event(k):
        for sign in (1, -1):
            dz = sign * (4 - (k + 2) // 2)
            first = 1 if sign > 0 else 0
            half = first if k % 2 == 1 else 1 - first
            reduce(sign, k).wait_recv()
            e = (0 if sign > 0 else 7) + k - 1
            add_into(part.at[slot(dz), pl.ds(half * HALF, HALF)], [rland.at[e]], HALF)
            reduce(sign, k + 2).start()

    lax.fori_loop(0, 3, weight_own, 0)
    gather_event(5)
    for sign in (1, -1):
        w_ring(sign).wait_recv()
        w_ring_far(sign).start()
    w_core(1).start()
    w_core(2).start()
    lax.fori_loop(3, 5, weight_own, 0)
    gp_copy(0).wait_recv()
    gp_copy(1).wait_recv()
    turn(1, 0)
    turn(1, 1)
    gather_event(6)
    lax.fori_loop(5, 7, weight_own, 0)

    w_ring_far(1).wait_recv()
    w_ring_far(-1).wait_recv()
    w_core(3).start()
    for n in range(8):
        w_load(n).wait()
    for i in range(4):
        w_core(i).wait_recv()
    lax.fori_loop(0, 3, share_far, 0)
    for k in (1, 2):
        reduce(1, k).start()
        reduce(-1, k).start()

    gather_event(7)
    lax.fori_loop(7, 8, weight_own, 0)
    lax.fori_loop(0, 3, sums_far, 0)

    def core_add(s, dy, dxh, more=()):
        o = dy * 2 + dxh
        core_copy(s, o).wait_recv()
        add_into(cland.at[s, o], [gsum.at[s, o, c], *more], GCOLS)

    def y_place(s, sign, dxh):
        return s * 4 + dxh * 2 + (0 if sign > 0 else 1)

    def y_half(s, sign, dxh):
        n = y_place(s, sign, dxh)
        half = 0 if sign > 0 else 1
        src = cland.at[s, 4 + dxh, pl.ds(half * GHALF, GHALF)]
        return remote(src, yhalf.at[n], y_s.at[n], y_r.at[n], at_y(sign))

    def y_full(s, sign, dxh):
        n = y_place(s, sign, dxh)
        src = cland.at[s, (2 if sign > 0 else 6) + dxh]
        return remote(src, yland.at[n], y_s.at[8 + n], y_r.at[8 + n], at_y(sign))

    def y_pass(s, dxh):
        for sign, dy, half in ((1, 1, 0), (-1, 3, 1)):
            n = y_place(s, sign, dxh)
            y_half(s, sign, dxh).wait_recv()
            add_into(cland.at[s, dy * 2 + dxh, pl.ds(half * GHALF, GHALF)], [yhalf.at[n]], GHALF)
            y_full(s, sign, dxh).start()

    def x_copy(n):
        src = cland.at[1, 1] if n == 4 else cland.at[0, n * 2 + 1]
        return remote(src, xland.at[n], x_s.at[n], x_r.at[n], at_xh)

    for dy in (2, 1):
        core_add(0, dy, 1)
        x_copy(dy).start()

    lax.fori_loop(0, 8, weight_cross, 0)
    core_add(1, 2, 1)
    y_half(1, 1, 1).start()
    y_half(1, -1, 1).start()
    reduce_event(1)
    core_add(1, 2, 0)
    y_half(1, 1, 0).start()
    y_half(1, -1, 0).start()
    core_add(0, 3, 1)
    x_copy(3).start()
    core_add(1, 1, 1)
    core_add(1, 3, 1)
    lax.fori_loop(0, 2, share_near, 0)
    y_pass(1, 1)
    reduce_event(2)
    lax.fori_loop(2, 5, share_near, 0)

    pack_rows(acc_a, st_send.at[1], 0)
    pack_rows(acc_b, st_send.at[1], 4)
    exchange_x(1).start()

    reduce_event(3)
    core_add(0, 0, 1)
    x_copy(0).start()
    core_add(1, 1, 0)
    core_add(1, 3, 0)
    y_pass(1, 0)
    exchange_x(1).wait_recv()
    sz_send[1] = st_send[1] + st_recv[1]
    for k in range(1, 8):
        exchange_z(1, k).start()
    core_add(1, 0, 1)
    core_add(1, 0, 0)
    reduce_event(4)

    y_full(1, 1, 1).wait_recv()
    y_full(1, -1, 1).wait_recv()
    add_into(cland.at[1, 1], [yland.at[6], yland.at[7]], GCOLS)
    x_copy(4).start()
    x_copy(2).wait_recv()
    core_add(0, 2, 0, [xland.at[2]])
    y_half(0, 1, 0).start()
    y_half(0, -1, 0).start()
    reduce_event(5)

    for dy in (1, 3):
        x_copy(dy).wait_recv()
        core_add(0, dy, 0, [xland.at[dy]])

    for k in range(1, 8):
        exchange_z(1, k).wait_recv()
    total = (sz_send[1] + sum(sz_recv[1, k] for k in range(1, 8))) / D
    spread_rows(total[0:4], acc_a)
    spread_rows(total[4:8], acc_b)

    owner_b = (y * 4 + xh * 2 + x, z * 2 + 1 - x)
    copy_b = remote(last.at[1], fin.at[c], f_s.at[1], f_r.at[c], owner_b)
    copy_a = remote(last.at[0], fin.at[c], f_s.at[0], f_r.at[c], at_c)

    def finish(s, sources):
        def step(r, carry):
            rows = pl.ds(pl.multiple_of(r * 64, 64), 64)
            total = cland[s, 0, rows, :].astype(F32)
            for source in sources:
                total = total + source[rows, :].astype(F32)
            last[s, rows, :] = total.astype(BF16)
            return carry

        lax.fori_loop(0, GCOLS // 64, step, 0)

    y_full(1, 1, 0).wait_recv()
    y_full(1, -1, 0).wait_recv()
    x_copy(4).wait_recv()
    finish(1, [yland.at[4], yland.at[5], xland.at[4]])
    copy_b.start()
    y_pass(0, 0)
    x_copy(0).wait_recv()
    core_add(0, 0, 0, [xland.at[0]])

    for k in (6, 7):
        reduce(1, k).wait_recv()
        reduce(-1, k).wait_recv()

    def in_step(r, carry):
        center, inverse = None, None
        for half in range(2):
            rows = pl.ds(pl.multiple_of(half * HALF + r * 64, 64), 64)
            inner = pl.ds(pl.multiple_of(r * 64, 64), 64)
            up, down = (5, 13) if half == 0 else (6, 12)
            center, inverse = mean_b[rows, :], inv_b[rows, :]
            plain, hat = acc_a[rows, :], acc_b[rows, :]
            for k in range(3):
                lanes = slice(k * LANES, (k + 1) * LANES)
                total = part[0, rows, lanes].astype(F32) + rland[up, inner, lanes].astype(F32)
                total = total + rland[down, inner, lanes].astype(F32)
                x_hat = (ag[0, rows, lanes].astype(F32) - center) * inverse
                scaled = total * gain[mp, :, lanes]
                gi_out[rows, lanes] = ((scaled - plain - x_hat * hat) * inverse).astype(BF16)
        return carry

    lax.fori_loop(0, HALF // 64, in_step, 0)

    y_full(0, 1, 0).wait_recv()
    y_full(0, -1, 0).wait_recv()
    finish(0, [yland.at[0], yland.at[1]])

    @pl.when(c == x)
    def _():
        fin[c] = last[0]
        remote(last.at[0], fin.at[1 - c], f_s.at[0], f_r.at[1 - c], at_c).wait_recv()

    @pl.when(c != x)
    def _():
        copy_a.start()
        for h in range(2):
            remote(last.at[1], fin.at[h], f_s.at[1], f_r.at[h], at_x).wait_recv()
        copy_a.wait_send()

    for h in range(2):
        for k in range(3):
            block = fin[h, k * HDIM : (k + 1) * HDIM, :].astype(F32)
            gw_out[k, :, h * HDIM : (h + 1) * HDIM] = block.T

    copy_b.wait_send()
    for sign in (1, -1):
        for k in range(1, 8):
            gather(sign, k).wait_send()
            reduce(sign, k).wait_send()
        for s, dxh in ((1, 1), (1, 0), (0, 0)):
            y_half(s, sign, dxh).wait_send()
            y_full(s, sign, dxh).wait_send()
    for n in range(2):
        gp_copy(n).wait_send()
        exchange_x(n).wait_send()
        for k in range(1, 8):
            exchange_z(n, k).wait_send()
        for o in range(8):
            core_copy(n, o).wait_send()
    w_cross().wait_send()
    for sign in (1, -1):
        w_ring(sign).wait_send()
        w_ring_far(sign).wait_send()
    for i in range(4):
        w_core(i).wait_send()
    for n in range(5):
        x_copy(n).wait_send()


def shards(tokens, ln_gain, projected, out_grad, w_joined):
    vmem = pltpu.VMEM
    dma = pltpu.SemaphoreType.DMA
    hbm = pl.BlockSpec(memory_space=pl.ANY)
    local = pl.BlockSpec(memory_space=pltpu.VMEM)
    grad_weight, grad_input = pl.pallas_call(
        kernel,
        out_shape=(
            jax.ShapeDtypeStruct((3, COLS, WIDTH), F32),
            jax.ShapeDtypeStruct((SEQ, COLS), BF16),
        ),
        in_specs=[hbm, local, hbm, hbm, hbm],
        out_specs=(local, local),
        scratch_shapes=[
            vmem((8, SEQ, COLS), BF16),
            vmem((8, 3, COLS, WIDTH), BF16),
            vmem((8, 3, COLS, WIDTH), BF16),
            vmem((3, SEQ, WIDTH), BF16),
            vmem((SEQ, WIDTH), BF16),
            vmem((2, 3, SEQ, WIDTH), BF16),
            vmem((2, 2, GCOLS, SEQ), BF16),
            vmem((8, SEQ, COLS), BF16),
            vmem((8, SEQ, COLS), BF16),
            vmem((14, HALF, COLS), BF16),
            vmem((2, 8, 2, GCOLS, COLS), BF16),
            vmem((2, 8, GCOLS, COLS), BF16),
            vmem((8, GCOLS, COLS), BF16),
            vmem((8, GHALF, COLS), BF16),
            vmem((5, GCOLS, COLS), BF16),
            vmem((2, GCOLS, COLS), BF16),
            vmem((2, GCOLS, COLS), BF16),
            vmem((SEQ, LANES), F32),
            vmem((SEQ, LANES), F32),
            vmem((SEQ, LANES), F32),
            vmem((SEQ, LANES), F32),
            vmem((2, 8, LANES), F32),
            vmem((2, 8, LANES), F32),
            vmem((2, 8, LANES), F32),
            vmem((2, 8, 8, LANES), F32),
            dma((3,)),
            dma((8,)),
            dma((14,)), dma((14,)),
            dma((2,)), dma((2,)),
            dma((2, 8)), dma((2, 8)),
            dma((5,)), dma((5,)),
            dma((4,)), dma((4,)),
            dma((2,)), dma((2,)),
            dma((14,)), dma((14,)),
            dma((2, 8)), dma((2, 8)),
            dma((16,)), dma((16,)),
            dma((5,)), dma((5,)),
            dma((2,)), dma((2,)),
        ],
        compiler_params=pltpu.CompilerParams(
            collective_id=0, has_side_effects=True, vmem_limit_bytes=62 * 1024 * 1024
        ),
        cost_estimate=pl.CostEstimate(flops=11_000_000_000, bytes_accessed=14_000_000, transcendentals=600_000),
        name="parallel_block_backward",
    )(
        tokens,
        ln_gain.reshape(16, 1, COLS),
        jnp.transpose(projected, (1, 0, 2)),
        out_grad,
        jnp.transpose(w_joined, (1, 0, 2)),
    )
    return jnp.transpose(grad_weight, (1, 0, 2)), grad_input


def solution(mesh):
    in_specs = (P("dp", "mp"), P(), P("dp", None, "mp"), P("dp", "mp"), P(None, None, "mp"))
    out_specs = (P("dp", None, "mp"), P("dp", "mp"))
    return jax.shard_map(shards, mesh=mesh, in_specs=in_specs, out_specs=out_specs, check_vma=False)
```

```python
import functools

import jax
import jax.numpy as jnp
from jax import lax
from jax.experimental import pallas as pl
from jax.experimental.pallas import tpu as pltpu
from jax.sharding import PartitionSpec as P

MESH = pl.DeviceIdType.MESH
F32 = jnp.float32
BF16 = jnp.bfloat16

D = 6144
HDIM = 128
SEQ = 512
COLS = 384
WIDTH = 256
HALF = SEQ // 2
GCOLS = 3 * HDIM
GHALF = GCOLS // 2
SCALE = HDIM ** (-0.5)
LANES = 128
LAST = None

NT = (((1,), (1,)), ((), ()))
NN = (((1,), (0,)), ((), ()))
TN = (((0,), (0,)), ((), ()))


def slot(dz):
    return 7 if abs(dz) == 4 else (2 * abs(dz) - (1 if dz < 0 else 0))


def dot(left, right, dims):
    return lax.dot_general(left, right, dims, preferred_element_type=F32)


def add_into(dst, sources, rows, chunk=64):
    def body(i, carry):
        at = pl.ds(pl.multiple_of(i * chunk, chunk), chunk)
        total = dst[at, :].astype(F32)
        for source in sources:
            total = total + source[at, :].astype(F32)
        dst[at, :] = total.astype(BF16)
        return carry

    lax.fori_loop(0, rows // chunk, body, 0)


def pack_rows(acc, out, first):
    for i in range(4):
        part = acc[i * LANES : (i + 1) * LANES, :]
        out[first + i : first + i + 1, :] = jnp.sum(part.T, axis=0, keepdims=True)


def spread_rows(rows, out):
    for i in range(4):
        out[i * LANES : (i + 1) * LANES, :] = jnp.broadcast_to(rows[i : i + 1, :], (LANES, LANES)).T


def kernel(
    tok, gain, proj, og, w, gw_out, gi_out,
    ag, wv, wx, pv, ov, gp, gpt, norm, part, rland, gsum, cland, yland, yhalf, xland, fin, last,
    acc_a, acc_b, mean_b, inv_b, st_send, st_recv, sz_send, sz_recv,
    load_sem, w_sem, ag_s, ag_r, st_s, st_r, sz_s, sz_r, wx_s, wx_r, wc_s, wc_r, gp_s, gp_r,
    rs_s, rs_r, c_s, c_r, y_s, y_r, x_s, x_r, f_s, f_r,
):
    dp, mp = lax.axis_index("dp"), lax.axis_index("mp")
    y, xh, c = dp // 4, (dp // 2) % 2, dp % 2
    z, x = mp // 2, mp % 2

    def at_z(k):
        return (dp, ((z + k + 8) % 8) * 2 + x)

    def at_y(k):
        return (((y + k + 4) % 4) * 4 + xh * 2 + c, mp)

    sibling = y * 4 + xh * 2 + 1 - c
    at_c = (sibling, mp)
    at_x = (dp, z * 2 + 1 - x)
    at_xc = (sibling, z * 2 + 1 - x)
    at_xh = (y * 4 + (1 - xh) * 2 + c, mp)
    at_xo = (y * 4 + (1 - xh) * 2 + c, z * 2 + 1 - x)

    def remote(src, dst, send, recv, device):
        return pltpu.make_async_remote_copy(
            src_ref=src, dst_ref=dst, send_sem=send, recv_sem=recv, device_id=device, device_id_type=MESH
        )

    def zed(n):
        return (z + ((n + 1) // 2) * (1 - 2 * (n % 2)) + 8) % 8

    def w_rows(n, column):
        return w.at[:, pl.ds(pl.multiple_of((zed(n) * 2 + column) * COLS, COLS), COLS), :]

    loads = [
        pltpu.make_async_copy(tok, ag.at[0], load_sem.at[0]),
        pltpu.make_async_copy(proj, pv, load_sem.at[1]),
        pltpu.make_async_copy(og, ov, load_sem.at[2]),
    ]
    for load in loads:
        load.start()

    def w_load(n):
        return pltpu.make_async_copy(w_rows(n, x), wv.at[n], w_sem.at[n])

    barrier = pltpu.get_barrier_semaphore()
    peers = [at_z(k) for k in range(1, 8)] + [at_c, at_x, at_xc, at_xh, at_xo, at_y(1), at_y(-1)]
    for peer in peers:
        pl.semaphore_signal(barrier, inc=1, device_id=peer, device_id_type=MESH)
    pl.semaphore_wait(barrier, len(peers))

    def gather(sign, k):
        hop = (k - 1) // 2
        half = (0 if sign > 0 else 1) if k % 2 == 1 else (1 if sign > 0 else 0)
        rows = pl.ds(half * HALF, HALF)
        src = tok.at[rows] if hop == 0 else ag.at[slot(-sign * hop), rows]
        e = (0 if sign > 0 else 7) + k - 1
        return remote(src, ag.at[slot(-sign * (hop + 1)), rows], ag_s.at[e], ag_r.at[e], at_z(sign))

    def gather_event(k):
        for sign in (1, -1):
            gather(sign, k).wait_recv()
            if k <= 5:
                gather(sign, k + 2).start()

    gather(1, 1).start()
    gather(-1, 1).start()

    def w_place(d, core):
        return 2 * ((y - d + 4) % 4) + 1 - core

    def w_cross():
        n = w_place(0, c)
        partner = (y * 4 + ((xh + c) % 2) * 2 + c, z * 2 + 1 - x)
        return remote(w_rows(n, 1 - x), wx.at[n], wx_s.at[0], wx_r.at[0], partner)

    def w_ring(sign, part):
        n = w_place(0, c)
        e = (1 if sign > 0 else 2) + 4 * part
        rows = pl.ds(0 if (sign > 0) == (part == 0) else COLS // 2, COLS // 2)
        return remote(wx.at[n, :, rows], wx.at[n, :, rows], wx_s.at[e], wx_r.at[e], at_y(sign))

    def w_ring_far(sign):
        n = w_place(sign, c)
        e = 3 if sign > 0 else 4
        rows = pl.ds(0 if sign > 0 else COLS // 2, COLS // 2)
        return remote(wx.at[n, :, rows], wx.at[n, :, rows], wx_s.at[e], wx_r.at[e], at_y(sign))

    def w_core(i):
        n = w_place((0, 1, -1, 2)[i], c)
        return remote(wx.at[n], wx.at[n], wc_s.at[i], wc_r.at[i], at_c)

    w_cross().start()
    for n in (7, 6, 5, 4, 3, 2, 1, 0):
        w_load(n).start()

    def exchange_x(n):
        return remote(st_send.at[n], st_recv.at[n], st_s.at[n], st_r.at[n], at_x)

    def exchange_z(n, k):
        return remote(sz_send.at[n], sz_recv.at[n, k], sz_s.at[n, k], sz_r.at[n, k], at_z(k))

    loads[0].wait()
    for i in range(4):
        rows = slice(i * LANES, (i + 1) * LANES)
        tiles = [ag[0, rows, k * LANES : (k + 1) * LANES].astype(F32) for k in range(3)]
        sums = tiles[0] + tiles[1] + tiles[2]
        center = jnp.sum(sums, axis=1, keepdims=True) / COLS
        acc_a[rows, :] = sums
        acc_b[rows, :] = sum(jnp.square(tile - center) for tile in tiles)
    pack_rows(acc_a, st_send.at[0], 0)
    pack_rows(acc_b, st_send.at[0], 4)
    st_send[0, 0:4, :] = st_send[0, 0:4, :] / COLS
    exchange_x(0).start()
    gather(1, 2).start()
    gather(-1, 2).start()

    def gp_copy(h):
        lanes = pl.ds(h * HDIM, HDIM)
        return remote(gp.at[0, :, :, lanes], gp.at[1, :, :, lanes], gp_s.at[h], gp_r.at[h], at_x)

    def head(h):
        cols = slice(h * HDIM, (h + 1) * HDIM)
        queries, keys_all, values, upstream = pv[0, :, cols], pv[1, :, cols], pv[2, :, cols], ov[:, cols]
        key_grad = value_grad = None
        for q0 in range(0, SEQ, 256):
            qs = slice(q0, q0 + 256)
            scores = dot(keys_all, queries[qs], NT) * SCALE
            raised = jnp.exp(scores - jnp.max(scores, axis=0, keepdims=True))
            probs = raised / jnp.sum(raised, axis=0, keepdims=True)
            term = dot(probs.astype(BF16), upstream[qs], NN)
            value_grad = term if value_grad is None else value_grad + term
            prob_grad = dot(values, upstream[qs], NT)
            score_grad = probs * (prob_grad - jnp.sum(probs * prob_grad, axis=0, keepdims=True))
            score_low = score_grad.astype(BF16)
            term = dot(score_low, queries[qs], NN)
            key_grad = term if key_grad is None else key_grad + term
            gp[0, 0, qs, cols] = (dot(score_low, keys_all, TN) * SCALE).astype(BF16)
        gp[0, 1, :, cols] = (key_grad * SCALE).astype(BF16)
        gp[0, 2, :, cols] = value_grad.astype(BF16)
        gp_copy(h).start()

    def turn(s, h):
        for k in range(3):
            gpt[s, h, k * HDIM : (k + 1) * HDIM, :] = gp[s, k, :, h * HDIM : (h + 1) * HDIM].T

    loads[1].wait()
    loads[2].wait()
    head(0)

    exchange_x(0).wait_recv()
    mine, other = st_send[0], st_recv[0]
    center = (mine[0:4] + other[0:4]) * 0.5
    sz_send[0, 0:4, :] = center
    sz_send[0, 4:8, :] = mine[4:8] + other[4:8] + COLS * (
        jnp.square(mine[0:4] - center) + jnp.square(other[0:4] - center)
    )
    for k in range(1, 8):
        exchange_z(0, k).start()

    gather_event(1)
    w_cross().wait_recv()
    w_ring(1, 0).start()
    w_ring(-1, 0).start()
    w_core(0).start()

    head(1)

    gather_event(2)
    w_ring(1, 1).start()
    w_ring(-1, 1).start()
    turn(0, 0)
    turn(0, 1)
    gather_event(3)
    for sign in (1, -1):
        w_ring(sign, 0).wait_recv()
        w_ring_far(sign).start()

    for k in range(1, 8):
        exchange_z(0, k).wait_recv()
    centers = [sz_send[0, 0:4, :]] + [sz_recv[0, k, 0:4, :] for k in range(1, 8)]
    squares = [sz_send[0, 4:8, :]] + [sz_recv[0, k, 4:8, :] for k in range(1, 8)]
    center = sum(centers) * 0.125
    spread = (sum(squares) + (2 * COLS) * sum(jnp.square(one - center) for one in centers)) / D
    spread_rows(center, mean_b)
    spread_rows(lax.rsqrt(spread + 1e-06), inv_b)
    gather_event(4)

    acc_a[...] = jnp.zeros_like(acc_a)
    acc_b[...] = jnp.zeros_like(acc_b)

    def core_copy(s, o):
        return remote(gsum.at[s, o, 1 - c], cland.at[s, o], c_s.at[s, o], c_r.at[s, o], at_c)

    def weight(s, n):
        o = ((zed(n) // 2 - y + 4) % 4) * 2 + (zed(n) + xh) % 2
        for h in range(2):
            gsum[s, o, h] = dot(gpt[s, h], norm[n], NN).astype(BF16)
        core_copy(s, o).start()

    def x_copy(n):
        src = cland.at[1, 1] if n is LAST else cland.at[0, n * 2 + 1]
        n = 4 if n is LAST else n
        return remote(src, xland.at[n], x_s.at[n], x_r.at[n], at_xh)

    def x_event(n):
        dy = (zed(n) // 2 - y + 4) % 4

        @pl.when((zed(n) + xh) % 2 == 1)
        def _():
            core_copy(0, dy * 2 + 1).wait_recv()
            add_into(cland.at[0, dy * 2 + 1], [gsum.at[0, dy * 2 + 1, c]], GCOLS)
            x_copy(dy).start()

    def weight_own(n, carry):
        j = zed(n) * 2 + x

        def rows_step(r, carry):
            rows = pl.ds(pl.multiple_of(r * 64, 64), 64)
            center, inverse = mean_b[rows, :], inv_b[rows, :]
            for k in range(3):
                lanes = slice(k * LANES, (k + 1) * LANES)
                value = (ag[n, rows, lanes].astype(F32) - center) * inverse * gain[j, :, lanes]
                norm[n, rows, lanes] = value.astype(BF16)
            return carry

        lax.fori_loop(0, SEQ // 64, rows_step, 0)
        weight(0, n)

        @pl.when(n > 0)
        def _():
            x_event(n - 1)

        return carry

    def weight_cross(n, carry):
        weight(1, n)
        return carry

    def share(n):
        for k in range(3):
            term = dot(gp[0, k], wv[n, k], NT) + dot(gp[1, k], wx[n, k], NT)
            total = term if k == 0 else total + term
        part[n] = total.astype(BF16)

    def sums(n):
        j = zed(n) * 2 + x

        def rows_step(r, carry):
            rows = pl.ds(pl.multiple_of(r * 64, 64), 64)
            plain, hat = acc_a[rows, :], acc_b[rows, :]
            for k in range(3):
                lanes = slice(k * LANES, (k + 1) * LANES)
                piece = part[n, rows, lanes].astype(F32)
                plain = plain + piece * gain[j, :, lanes]
                hat = hat + piece * norm[n, rows, lanes].astype(F32)
            acc_a[rows, :] = plain
            acc_b[rows, :] = hat
            return carry

        lax.fori_loop(0, SEQ // 64, rows_step, 0)

    def share_far(i, carry):
        share(7 - i)
        return carry

    def share_near(i, carry):
        share(4 - i)
        sums(4 - i)
        return carry

    def sums_far(i, carry):
        sums(7 - i)
        return carry

    def reduce(sign, k):
        dz = sign * (4 - k // 2)
        first = 1 if sign > 0 else 0
        half = first if k % 2 == 1 else 1 - first
        e = (0 if sign > 0 else 7) + k - 1
        return remote(
            part.at[slot(dz), pl.ds(half * HALF, HALF)], rland.at[e], rs_s.at[e], rs_r.at[e], at_z(sign)
        )

    def reduce_event(k):
        for sign in (1, -1):
            dz = sign * (4 - (k + 2) // 2)
            first = 1 if sign > 0 else 0
            half = first if k % 2 == 1 else 1 - first
            reduce(sign, k).wait_recv()
            e = (0 if sign > 0 else 7) + k - 1
            add_into(part.at[slot(dz), pl.ds(half * HALF, HALF)], [rland.at[e]], HALF)
            reduce(sign, k + 2).start()

    lax.fori_loop(0, 3, weight_own, 0)
    gather_event(5)
    w_ring(1, 1).wait_recv()
    w_ring(-1, 1).wait_recv()
    w_core(1).start()
    w_core(2).start()
    lax.fori_loop(3, 5, weight_own, 0)
    gp_copy(0).wait_recv()
    gp_copy(1).wait_recv()
    turn(1, 0)
    turn(1, 1)
    gather_event(6)
    lax.fori_loop(5, 7, weight_own, 0)
    lax.fori_loop(0, 5, weight_cross, 0)

    w_ring_far(1).wait_recv()
    w_ring_far(-1).wait_recv()
    w_core(3).start()
    for n in range(8):
        w_load(n).wait()
    for i in range(4):
        w_core(i).wait_recv()
    lax.fori_loop(0, 3, share_far, 0)
    reduce(1, 1).start()
    reduce(-1, 1).start()

    gather_event(7)
    lax.fori_loop(7, 8, weight_own, 0)
    x_event(7)
    lax.fori_loop(5, 8, weight_cross, 0)
    reduce(1, 2).start()
    reduce(-1, 2).start()

    def core_add(s, dy, dxh, more=()):
        o = dy * 2 + dxh
        core_copy(s, o).wait_recv()
        add_into(cland.at[s, o], [gsum.at[s, o, c], *more], GCOLS)

    def y_place(s, sign, dxh):
        return s * 4 + dxh * 2 + (0 if sign > 0 else 1)

    def y_half(s, sign, dxh):
        n = y_place(s, sign, dxh)
        half = 0 if sign > 0 else 1
        src = cland.at[s, 4 + dxh, pl.ds(half * GHALF, GHALF)]
        return remote(src, yhalf.at[n], y_s.at[n], y_r.at[n], at_y(sign))

    def y_full(s, sign, dxh):
        n = y_place(s, sign, dxh)
        src = cland.at[s, (2 if sign > 0 else 6) + dxh]
        return remote(src, yland.at[n], y_s.at[8 + n], y_r.at[8 + n], at_y(sign))

    def y_pass(s, dxh):
        for sign, dy, half in ((1, 1, 0), (-1, 3, 1)):
            n = y_place(s, sign, dxh)
            y_half(s, sign, dxh).wait_recv()
            add_into(cland.at[s, dy * 2 + dxh, pl.ds(half * GHALF, GHALF)], [yhalf.at[n]], GHALF)
            y_full(s, sign, dxh).start()

    core_add(1, 2, 1)
    y_half(1, 1, 1).start()
    y_half(1, -1, 1).start()
    lax.fori_loop(0, 3, sums_far, 0)
    reduce_event(1)
    core_add(1, 2, 0)
    y_half(1, 1, 0).start()
    y_half(1, -1, 0).start()
    core_add(1, 1, 1)
    core_add(1, 3, 1)
    lax.fori_loop(0, 2, share_near, 0)
    y_pass(1, 1)
    reduce_event(2)
    lax.fori_loop(2, 5, share_near, 0)

    pack_rows(acc_a, st_send.at[1], 0)
    pack_rows(acc_b, st_send.at[1], 4)
    exchange_x(1).start()

    reduce_event(3)
    core_add(1, 1, 0)
    core_add(1, 3, 0)
    y_pass(1, 0)
    exchange_x(1).wait_recv()
    sz_send[1] = st_send[1] + st_recv[1]
    for k in range(1, 8):
        exchange_z(1, k).start()
    core_add(1, 0, 1)
    core_add(1, 0, 0)
    reduce_event(4)

    y_full(1, 1, 1).wait_recv()
    y_full(1, -1, 1).wait_recv()
    add_into(cland.at[1, 1], [yland.at[6], yland.at[7]], GCOLS)
    x_copy(LAST).start()
    x_copy(2).wait_recv()
    core_add(0, 2, 0, [xland.at[2]])
    y_half(0, 1, 0).start()
    y_half(0, -1, 0).start()
    reduce_event(5)

    for dy in (1, 3):
        x_copy(dy).wait_recv()
        core_add(0, dy, 0, [xland.at[dy]])

    for k in range(1, 8):
        exchange_z(1, k).wait_recv()
    total = (sz_send[1] + sum(sz_recv[1, k] for k in range(1, 8))) / D
    spread_rows(total[0:4], acc_a)
    spread_rows(total[4:8], acc_b)

    owner_b = (y * 4 + xh * 2 + x, z * 2 + 1 - x)
    copy_b = remote(last.at[1], fin.at[c], f_s.at[1], f_r.at[c], owner_b)
    copy_a = remote(last.at[0], fin.at[c], f_s.at[0], f_r.at[c], at_c)

    def finish(s, sources):
        def step(r, carry):
            rows = pl.ds(pl.multiple_of(r * 64, 64), 64)
            total = cland[s, 0, rows, :].astype(F32)
            for source in sources:
                total = total + source[rows, :].astype(F32)
            last[s, rows, :] = total.astype(BF16)
            return carry

        lax.fori_loop(0, GCOLS // 64, step, 0)

    y_full(1, 1, 0).wait_recv()
    y_full(1, -1, 0).wait_recv()
    x_copy(LAST).wait_recv()
    finish(1, [yland.at[4], yland.at[5], xland.at[4]])
    copy_b.start()
    y_pass(0, 0)
    x_copy(0).wait_recv()
    core_add(0, 0, 0, [xland.at[0]])

    for k in (6, 7):
        reduce(1, k).wait_recv()
        reduce(-1, k).wait_recv()

    def in_step(r, carry):
        center, inverse = None, None
        for half in range(2):
            rows = pl.ds(pl.multiple_of(half * HALF + r * 64, 64), 64)
            inner = pl.ds(pl.multiple_of(r * 64, 64), 64)
            up, down = (5, 13) if half == 0 else (6, 12)
            center, inverse = mean_b[rows, :], inv_b[rows, :]
            plain, hat = acc_a[rows, :], acc_b[rows, :]
            for k in range(3):
                lanes = slice(k * LANES, (k + 1) * LANES)
                total = part[0, rows, lanes].astype(F32) + rland[up, inner, lanes].astype(F32)
                total = total + rland[down, inner, lanes].astype(F32)
                x_hat = (ag[0, rows, lanes].astype(F32) - center) * inverse
                scaled = total * gain[mp, :, lanes]
                gi_out[rows, lanes] = ((scaled - plain - x_hat * hat) * inverse).astype(BF16)
        return carry

    lax.fori_loop(0, HALF // 64, in_step, 0)

    y_full(0, 1, 0).wait_recv()
    y_full(0, -1, 0).wait_recv()
    finish(0, [yland.at[0], yland.at[1]])

    @pl.when(c == x)
    def _():
        fin[c] = last[0]
        remote(last.at[0], fin.at[1 - c], f_s.at[0], f_r.at[1 - c], at_c).wait_recv()

    @pl.when(c != x)
    def _():
        copy_a.start()
        for h in range(2):
            remote(last.at[1], fin.at[h], f_s.at[1], f_r.at[h], at_x).wait_recv()
        copy_a.wait_send()

    for h in range(2):
        for k in range(3):
            block = fin[h, k * HDIM : (k + 1) * HDIM, :].astype(F32)
            gw_out[k, :, h * HDIM : (h + 1) * HDIM] = block.T

    copy_b.wait_send()
    for sign in (1, -1):
        for k in range(1, 8):
            gather(sign, k).wait_send()
            reduce(sign, k).wait_send()
        for s, dxh in ((1, 1), (1, 0), (0, 0)):
            y_half(s, sign, dxh).wait_send()
            y_full(s, sign, dxh).wait_send()
    for n in range(2):
        gp_copy(n).wait_send()
        exchange_x(n).wait_send()
        for k in range(1, 8):
            exchange_z(n, k).wait_send()
        for o in range(8):
            core_copy(n, o).wait_send()
    w_cross().wait_send()
    for sign in (1, -1):
        w_ring(sign, 0).wait_send()
        w_ring(sign, 1).wait_send()
        w_ring_far(sign).wait_send()
    for i in range(4):
        w_core(i).wait_send()
    for n in (0, 1, 2, 3, LAST):
        x_copy(n).wait_send()


def shards(tokens, ln_gain, projected, out_grad, w_joined):
    vmem = pltpu.VMEM
    dma = pltpu.SemaphoreType.DMA
    hbm = pl.BlockSpec(memory_space=pl.ANY)
    local = pl.BlockSpec(memory_space=pltpu.VMEM)
    grad_weight, grad_input = pl.pallas_call(
        kernel,
        out_shape=(
            jax.ShapeDtypeStruct((3, COLS, WIDTH), F32),
            jax.ShapeDtypeStruct((SEQ, COLS), BF16),
        ),
        in_specs=[hbm, local, hbm, hbm, hbm],
        out_specs=(local, local),
        scratch_shapes=[
            vmem((8, SEQ, COLS), BF16),
            vmem((8, 3, COLS, WIDTH), BF16),
            vmem((8, 3, COLS, WIDTH), BF16),
            vmem((3, SEQ, WIDTH), BF16),
            vmem((SEQ, WIDTH), BF16),
            vmem((2, 3, SEQ, WIDTH), BF16),
            vmem((2, 2, GCOLS, SEQ), BF16),
            vmem((8, SEQ, COLS), BF16),
            vmem((8, SEQ, COLS), BF16),
            vmem((14, HALF, COLS), BF16),
            vmem((2, 8, 2, GCOLS, COLS), BF16),
            vmem((2, 8, GCOLS, COLS), BF16),
            vmem((8, GCOLS, COLS), BF16),
            vmem((8, GHALF, COLS), BF16),
            vmem((5, GCOLS, COLS), BF16),
            vmem((2, GCOLS, COLS), BF16),
            vmem((2, GCOLS, COLS), BF16),
            vmem((SEQ, LANES), F32),
            vmem((SEQ, LANES), F32),
            vmem((SEQ, LANES), F32),
            vmem((SEQ, LANES), F32),
            vmem((2, 8, LANES), F32),
            vmem((2, 8, LANES), F32),
            vmem((2, 8, LANES), F32),
            vmem((2, 8, 8, LANES), F32),
            dma((3,)),
            dma((8,)),
            dma((14,)), dma((14,)),
            dma((2,)), dma((2,)),
            dma((2, 8)), dma((2, 8)),
            dma((7,)), dma((7,)),
            dma((4,)), dma((4,)),
            dma((2,)), dma((2,)),
            dma((14,)), dma((14,)),
            dma((2, 8)), dma((2, 8)),
            dma((16,)), dma((16,)),
            dma((5,)), dma((5,)),
            dma((2,)), dma((2,)),
        ],
        compiler_params=pltpu.CompilerParams(
            collective_id=0, has_side_effects=True, vmem_limit_bytes=62 * 1024 * 1024
        ),
        cost_estimate=pl.CostEstimate(flops=11_000_000_000, bytes_accessed=14_000_000, transcendentals=600_000),
        name="parallel_block_backward",
    )(
        tokens,
        ln_gain.reshape(16, 1, COLS),
        jnp.transpose(projected, (1, 0, 2)),
        out_grad,
        jnp.transpose(w_joined, (1, 0, 2)),
    )
    return jnp.transpose(grad_weight, (1, 0, 2)), grad_input


def solution(mesh):
    in_specs = (P("dp", "mp"), P(), P("dp", None, "mp"), P("dp", "mp"), P(None, None, "mp"))
    out_specs = (P("dp", None, "mp"), P("dp", "mp"))
    return jax.shard_map(shards, mesh=mesh, in_specs=in_specs, out_specs=out_specs, check_vma=False)
```

```python
import functools

import jax
import jax.numpy as jnp
from jax import lax
from jax.experimental import pallas as pl
from jax.experimental.pallas import tpu as pltpu
from jax.sharding import PartitionSpec as P

MESH = pl.DeviceIdType.MESH
F32 = jnp.float32
BF16 = jnp.bfloat16

D = 6144
HDIM = 128
SEQ = 512
COLS = 384
WIDTH = 256
HALF = SEQ // 2
GCOLS = 3 * HDIM
GHALF = GCOLS // 2
SCALE = HDIM ** (-0.5)
LANES = 128
LAST = None

NT = (((1,), (1,)), ((), ()))
NN = (((1,), (0,)), ((), ()))
TN = (((0,), (0,)), ((), ()))


def slot(dz):
    return 7 if abs(dz) == 4 else (2 * abs(dz) - (1 if dz < 0 else 0))


def dot(left, right, dims):
    return lax.dot_general(left, right, dims, preferred_element_type=F32)


def add_into(dst, sources, rows, chunk=64):
    def body(i, carry):
        at = pl.ds(pl.multiple_of(i * chunk, chunk), chunk)
        total = dst[at, :].astype(F32)
        for source in sources:
            total = total + source[at, :].astype(F32)
        dst[at, :] = total.astype(BF16)
        return carry

    lax.fori_loop(0, rows // chunk, body, 0)


def pack_rows(acc, out, first):
    for i in range(4):
        part = acc[i * LANES : (i + 1) * LANES, :]
        out[first + i : first + i + 1, :] = jnp.sum(part.T, axis=0, keepdims=True)


def spread_rows(rows, out):
    for i in range(4):
        out[i * LANES : (i + 1) * LANES, :] = jnp.broadcast_to(rows[i : i + 1, :], (LANES, LANES)).T


def kernel(
    tok, gain, proj, og, w, gw_out, gi_out,
    ag, wv, wx, pv, ov, gp, gpt, norm, part, rland, gsum, cland, yland, yhalf, xland, fin, last,
    acc_a, acc_b, mean_b, inv_b, st_send, st_recv, sz_send, sz_recv,
    load_sem, w_sem, ag_s, ag_r, st_s, st_r, sz_s, sz_r, wx_s, wx_r, wc_s, wc_r, gp_s, gp_r,
    rs_s, rs_r, c_s, c_r, y_s, y_r, x_s, x_r, f_s, f_r,
):
    dp, mp = lax.axis_index("dp"), lax.axis_index("mp")
    y, xh, c = dp // 4, (dp // 2) % 2, dp % 2
    z, x = mp // 2, mp % 2

    def at_z(k):
        return (dp, ((z + k + 8) % 8) * 2 + x)

    def at_y(k):
        return (((y + k + 4) % 4) * 4 + xh * 2 + c, mp)

    sibling = y * 4 + xh * 2 + 1 - c
    at_c = (sibling, mp)
    at_x = (dp, z * 2 + 1 - x)
    at_xc = (sibling, z * 2 + 1 - x)
    at_xh = (y * 4 + (1 - xh) * 2 + c, mp)
    at_xo = (y * 4 + (1 - xh) * 2 + c, z * 2 + 1 - x)

    def remote(src, dst, send, recv, device):
        return pltpu.make_async_remote_copy(
            src_ref=src, dst_ref=dst, send_sem=send, recv_sem=recv, device_id=device, device_id_type=MESH
        )

    def zed(n):
        return (z + ((n + 1) // 2) * (1 - 2 * (n % 2)) + 8) % 8

    def w_rows(n, column):
        return w.at[:, pl.ds(pl.multiple_of((zed(n) * 2 + column) * COLS, COLS), COLS), :]

    loads = [
        pltpu.make_async_copy(tok, ag.at[0], load_sem.at[0]),
        pltpu.make_async_copy(proj, pv, load_sem.at[1]),
        pltpu.make_async_copy(og, ov, load_sem.at[2]),
    ]
    for load in loads:
        load.start()

    def w_load(n):
        return pltpu.make_async_copy(w_rows(n, x), wv.at[n], w_sem.at[n])

    barrier = pltpu.get_barrier_semaphore()
    peers = [at_z(k) for k in range(1, 8)] + [at_c, at_x, at_xc, at_xh, at_xo, at_y(1), at_y(-1)]
    for peer in peers:
        pl.semaphore_signal(barrier, inc=1, device_id=peer, device_id_type=MESH)
    pl.semaphore_wait(barrier, len(peers))

    def gather(sign, k):
        hop = (k - 1) // 2
        half = (0 if sign > 0 else 1) if k % 2 == 1 else (1 if sign > 0 else 0)
        rows = pl.ds(half * HALF, HALF)
        src = tok.at[rows] if hop == 0 else ag.at[slot(-sign * hop), rows]
        e = (0 if sign > 0 else 7) + k - 1
        return remote(src, ag.at[slot(-sign * (hop + 1)), rows], ag_s.at[e], ag_r.at[e], at_z(sign))

    def gather_event(k):
        for sign in (1, -1):
            gather(sign, k).wait_recv()
            if k <= 5:
                gather(sign, k + 2).start()

    gather(1, 1).start()
    gather(-1, 1).start()

    def w_place(d, core):
        return 2 * ((y - d + 4) % 4) + 1 - core

    def w_cross():
        n = w_place(0, c)
        partner = (y * 4 + ((xh + c) % 2) * 2 + c, z * 2 + 1 - x)
        return remote(w_rows(n, 1 - x), wx.at[n], wx_s.at[0], wx_r.at[0], partner)

    def w_ring(sign, part):
        n = w_place(0, c)
        e = (1 if sign > 0 else 2) + 4 * part
        rows = pl.ds(0 if (sign > 0) == (part == 0) else COLS // 2, COLS // 2)
        return remote(wx.at[n, :, rows], wx.at[n, :, rows], wx_s.at[e], wx_r.at[e], at_y(sign))

    def w_ring_far(sign):
        n = w_place(sign, c)
        e = 3 if sign > 0 else 4
        rows = pl.ds(0 if sign > 0 else COLS // 2, COLS // 2)
        return remote(wx.at[n, :, rows], wx.at[n, :, rows], wx_s.at[e], wx_r.at[e], at_y(sign))

    def w_core(i):
        n = w_place((0, 1, -1, 2)[i], c)
        return remote(wx.at[n], wx.at[n], wc_s.at[i], wc_r.at[i], at_c)

    w_cross().start()
    for n in (7, 6, 5, 4, 3, 2, 1, 0):
        w_load(n).start()

    def exchange_x(n):
        return remote(st_send.at[n], st_recv.at[n], st_s.at[n], st_r.at[n], at_x)

    def exchange_z(n, k):
        return remote(sz_send.at[n], sz_recv.at[n, k], sz_s.at[n, k], sz_r.at[n, k], at_z(k))

    loads[0].wait()
    for i in range(4):
        rows = slice(i * LANES, (i + 1) * LANES)
        tiles = [ag[0, rows, k * LANES : (k + 1) * LANES].astype(F32) for k in range(3)]
        sums = tiles[0] + tiles[1] + tiles[2]
        center = jnp.sum(sums, axis=1, keepdims=True) / COLS
        acc_a[rows, :] = sums
        acc_b[rows, :] = sum(jnp.square(tile - center) for tile in tiles)
    pack_rows(acc_a, st_send.at[0], 0)
    pack_rows(acc_b, st_send.at[0], 4)
    st_send[0, 0:4, :] = st_send[0, 0:4, :] / COLS
    exchange_x(0).start()
    gather(1, 2).start()
    gather(-1, 2).start()

    def gp_copy(h):
        lanes = pl.ds(h * HDIM, HDIM)
        return remote(gp.at[0, :, :, lanes], gp.at[1, :, :, lanes], gp_s.at[h], gp_r.at[h], at_x)

    def head(h):
        cols = slice(h * HDIM, (h + 1) * HDIM)
        queries, keys_all, values, upstream = pv[0, :, cols], pv[1, :, cols], pv[2, :, cols], ov[:, cols]
        key_grad = value_grad = None
        for q0 in range(0, SEQ, 256):
            qs = slice(q0, q0 + 256)
            scores = dot(keys_all, queries[qs], NT) * SCALE
            raised = jnp.exp(scores - jnp.max(scores, axis=0, keepdims=True))
            probs = raised / jnp.sum(raised, axis=0, keepdims=True)
            term = dot(probs.astype(BF16), upstream[qs], NN)
            value_grad = term if value_grad is None else value_grad + term
            prob_grad = dot(values, upstream[qs], NT)
            score_grad = probs * (prob_grad - jnp.sum(probs * prob_grad, axis=0, keepdims=True))
            score_low = score_grad.astype(BF16)
            term = dot(score_low, queries[qs], NN)
            key_grad = term if key_grad is None else key_grad + term
            gp[0, 0, qs, cols] = (dot(score_low, keys_all, TN) * SCALE).astype(BF16)
        gp[0, 1, :, cols] = (key_grad * SCALE).astype(BF16)
        gp[0, 2, :, cols] = value_grad.astype(BF16)
        gp_copy(h).start()

    def turn(s, h):
        for k in range(3):
            first = h * GCOLS + k * HDIM
            gpt[s, first : first + HDIM, :] = gp[s, k, :, h * HDIM : (h + 1) * HDIM].T

    loads[1].wait()
    loads[2].wait()
    head(0)

    exchange_x(0).wait_recv()
    mine, other = st_send[0], st_recv[0]
    center = (mine[0:4] + other[0:4]) * 0.5
    sz_send[0, 0:4, :] = center
    sz_send[0, 4:8, :] = mine[4:8] + other[4:8] + COLS * (
        jnp.square(mine[0:4] - center) + jnp.square(other[0:4] - center)
    )
    for k in range(1, 8):
        exchange_z(0, k).start()

    gather_event(1)
    w_cross().wait_recv()
    w_ring(1, 0).start()
    w_ring(-1, 0).start()
    w_core(0).start()

    head(1)

    gather_event(2)
    w_ring(1, 1).start()
    w_ring(-1, 1).start()
    turn(0, 0)
    turn(0, 1)
    gather_event(3)
    for sign in (1, -1):
        w_ring(sign, 0).wait_recv()
        w_ring_far(sign).start()

    for k in range(1, 8):
        exchange_z(0, k).wait_recv()
    centers = [sz_send[0, 0:4, :]] + [sz_recv[0, k, 0:4, :] for k in range(1, 8)]
    squares = [sz_send[0, 4:8, :]] + [sz_recv[0, k, 4:8, :] for k in range(1, 8)]
    center = sum(centers) * 0.125
    spread = (sum(squares) + (2 * COLS) * sum(jnp.square(one - center) for one in centers)) / D
    spread_rows(center, mean_b)
    spread_rows(lax.rsqrt(spread + 1e-06), inv_b)
    gather_event(4)

    acc_a[...] = jnp.zeros_like(acc_a)
    acc_b[...] = jnp.zeros_like(acc_b)

    def head_rows(core):
        return pl.ds(pl.multiple_of(core * GCOLS, GCOLS), GCOLS)

    def core_copy(s, o):
        return remote(gsum.at[s, o, head_rows(1 - c)], cland.at[s, o], c_s.at[s, o], c_r.at[s, o], at_c)

    def weight(s, n):
        o = ((zed(n) // 2 - y + 4) % 4) * 2 + (zed(n) + xh) % 2
        gsum[s, o] = dot(gpt[s], norm[n], NN).astype(BF16)
        core_copy(s, o).start()

    def x_copy(n):
        src = cland.at[1, 1] if n is LAST else cland.at[0, n * 2 + 1]
        n = 4 if n is LAST else n
        return remote(src, xland.at[n], x_s.at[n], x_r.at[n], at_xh)

    def x_event(n):
        dy = (zed(n) // 2 - y + 4) % 4

        @pl.when((zed(n) + xh) % 2 == 1)
        def _():
            core_copy(0, dy * 2 + 1).wait_recv()
            add_into(cland.at[0, dy * 2 + 1], [gsum.at[0, dy * 2 + 1, head_rows(c)]], GCOLS)
            x_copy(dy).start()

    def normalize(n):
        j = zed(n) * 2 + x

        def rows_step(r, carry):
            rows = pl.ds(pl.multiple_of(r * 64, 64), 64)
            center, inverse = mean_b[rows, :], inv_b[rows, :]
            for k in range(3):
                lanes = slice(k * LANES, (k + 1) * LANES)
                value = (ag[n, rows, lanes].astype(F32) - center) * inverse * gain[j, :, lanes]
                norm[n, rows, lanes] = value.astype(BF16)
            return carry

        lax.fori_loop(0, SEQ // 64, rows_step, 0)

    def weight_own(n, carry):
        normalize(n)
        weight(0, n)

        @pl.when(n > 4)
        def _():
            x_event(n - 1)

        return carry

    def x_step(n, carry):
        x_event(n)
        return carry

    def weight_cross(n, carry):
        weight(1, n)
        return carry

    def share(n):
        for k in range(3):
            term = dot(gp[0, k], wv[n, k], NT) + dot(gp[1, k], wx[n, k], NT)
            total = term if k == 0 else total + term
        part[n] = total.astype(BF16)

    def sums(n):
        j = zed(n) * 2 + x

        def rows_step(r, carry):
            rows = pl.ds(pl.multiple_of(r * 64, 64), 64)
            plain, hat = acc_a[rows, :], acc_b[rows, :]
            for k in range(3):
                lanes = slice(k * LANES, (k + 1) * LANES)
                piece = part[n, rows, lanes].astype(F32)
                plain = plain + piece * gain[j, :, lanes]
                hat = hat + piece * norm[n, rows, lanes].astype(F32)
            acc_a[rows, :] = plain
            acc_b[rows, :] = hat
            return carry

        lax.fori_loop(0, SEQ // 64, rows_step, 0)

    def share_near(i, carry):
        share(4 - i)
        sums(4 - i)
        return carry

    def sums_step(n, carry):
        sums(n)
        return carry

    def reduce(sign, k):
        dz = sign * (4 - k // 2)
        first = 1 if sign > 0 else 0
        half = first if k % 2 == 1 else 1 - first
        e = (0 if sign > 0 else 7) + k - 1
        return remote(
            part.at[slot(dz), pl.ds(half * HALF, HALF)], rland.at[e], rs_s.at[e], rs_r.at[e], at_z(sign)
        )

    def reduce_event(k):
        for sign in (1, -1):
            dz = sign * (4 - (k + 2) // 2)
            first = 1 if sign > 0 else 0
            half = first if k % 2 == 1 else 1 - first
            reduce(sign, k).wait_recv()
            e = (0 if sign > 0 else 7) + k - 1
            add_into(part.at[slot(dz), pl.ds(half * HALF, HALF)], [rland.at[e]], HALF)
            reduce(sign, k + 2).start()

    lax.fori_loop(0, 3, weight_own, 0)
    gather_event(5)
    w_ring(1, 1).wait_recv()
    w_ring(-1, 1).wait_recv()
    w_core(1).start()
    w_core(2).start()
    lax.fori_loop(3, 5, weight_own, 0)
    gp_copy(0).wait_recv()
    gp_copy(1).wait_recv()
    lax.fori_loop(0, 4, x_step, 0)
    turn(1, 0)
    turn(1, 1)
    gather_event(6)
    lax.fori_loop(5, 7, weight_own, 0)
    lax.fori_loop(0, 5, weight_cross, 0)

    w_ring_far(1).wait_recv()
    w_ring_far(-1).wait_recv()
    w_core(3).start()
    for n in range(8):
        w_load(n).wait()
    for i in range(4):
        w_core(i).wait_recv()
    share(7)
    reduce(1, 1).start()
    reduce(-1, 1).start()
    share(6)
    reduce(1, 2).start()
    share(5)
    reduce(-1, 2).start()
    gather_event(7)
    normalize(7)
    lax.fori_loop(5, 8, weight_cross, 0)
    weight(0, 7)

    def core_add(s, dy, dxh, more=()):
        o = dy * 2 + dxh
        core_copy(s, o).wait_recv()
        add_into(cland.at[s, o], [gsum.at[s, o, head_rows(c)], *more], GCOLS)

    def y_place(s, sign, dxh):
        return s * 4 + dxh * 2 + (0 if sign > 0 else 1)

    def y_half(s, sign, dxh):
        n = y_place(s, sign, dxh)
        half = 0 if sign > 0 else 1
        src = cland.at[s, 4 + dxh, pl.ds(half * GHALF, GHALF)]
        return remote(src, yhalf.at[n], y_s.at[n], y_r.at[n], at_y(sign))

    def y_full(s, sign, dxh):
        n = y_place(s, sign, dxh)
        src = cland.at[s, (2 if sign > 0 else 6) + dxh]
        return remote(src, yland.at[n], y_s.at[8 + n], y_r.at[8 + n], at_y(sign))

    def y_pass(s, dxh):
        for sign, dy, half in ((1, 1, 0), (-1, 3, 1)):
            n = y_place(s, sign, dxh)
            y_half(s, sign, dxh).wait_recv()
            add_into(cland.at[s, dy * 2 + dxh, pl.ds(half * GHALF, GHALF)], [yhalf.at[n]], GHALF)
            y_full(s, sign, dxh).start()

    core_add(1, 2, 1)
    y_half(1, 1, 1).start()
    y_half(1, -1, 1).start()
    lax.fori_loop(6, 8, x_step, 0)
    lax.fori_loop(5, 8, sums_step, 0)
    reduce_event(1)
    lax.fori_loop(0, 2, share_near, 0)
    reduce_event(2)
    core_add(1, 2, 0)
    y_half(1, 1, 0).start()
    y_half(1, -1, 0).start()
    core_add(1, 1, 1)
    core_add(1, 3, 1)
    y_pass(1, 1)
    reduce_event(3)
    lax.fori_loop(2, 5, share_near, 0)

    pack_rows(acc_a, st_send.at[1], 0)
    pack_rows(acc_b, st_send.at[1], 4)
    exchange_x(1).start()

    reduce_event(4)
    core_add(1, 1, 0)
    core_add(1, 3, 0)
    y_pass(1, 0)
    exchange_x(1).wait_recv()
    sz_send[1] = st_send[1] + st_recv[1]
    for k in range(1, 8):
        exchange_z(1, k).start()
    core_add(1, 0, 1)
    core_add(1, 0, 0)

    y_full(1, 1, 1).wait_recv()
    y_full(1, -1, 1).wait_recv()
    add_into(cland.at[1, 1], [yland.at[6], yland.at[7]], GCOLS)
    x_copy(LAST).start()
    x_copy(2).wait_recv()
    core_add(0, 2, 0, [xland.at[2]])
    y_half(0, 1, 0).start()
    y_half(0, -1, 0).start()
    reduce_event(5)

    for dy in (1, 3):
        x_copy(dy).wait_recv()
        core_add(0, dy, 0, [xland.at[dy]])

    for k in range(1, 8):
        exchange_z(1, k).wait_recv()
    total = (sz_send[1] + sum(sz_recv[1, k] for k in range(1, 8))) / D
    spread_rows(total[0:4], acc_a)
    spread_rows(total[4:8], acc_b)

    owner_b = (y * 4 + xh * 2 + x, z * 2 + 1 - x)
    copy_b = remote(last.at[1], fin.at[c], f_s.at[1], f_r.at[c], owner_b)
    copy_a = remote(last.at[0], fin.at[c], f_s.at[0], f_r.at[c], at_c)

    def finish(s, sources):
        def step(r, carry):
            rows = pl.ds(pl.multiple_of(r * 64, 64), 64)
            total = cland[s, 0, rows, :].astype(F32)
            for source in sources:
                total = total + source[rows, :].astype(F32)
            last[s, rows, :] = total.astype(BF16)
            return carry

        lax.fori_loop(0, GCOLS // 64, step, 0)

    y_full(1, 1, 0).wait_recv()
    y_full(1, -1, 0).wait_recv()
    x_copy(LAST).wait_recv()
    finish(1, [yland.at[4], yland.at[5], xland.at[4]])
    copy_b.start()
    y_pass(0, 0)
    x_copy(0).wait_recv()
    core_add(0, 0, 0, [xland.at[0]])

    for k in (6, 7):
        reduce(1, k).wait_recv()
        reduce(-1, k).wait_recv()

    def in_step(r, carry):
        center, inverse = None, None
        for half in range(2):
            rows = pl.ds(pl.multiple_of(half * HALF + r * 64, 64), 64)
            inner = pl.ds(pl.multiple_of(r * 64, 64), 64)
            up, down = (5, 13) if half == 0 else (6, 12)
            center, inverse = mean_b[rows, :], inv_b[rows, :]
            plain, hat = acc_a[rows, :], acc_b[rows, :]
            for k in range(3):
                lanes = slice(k * LANES, (k + 1) * LANES)
                total = part[0, rows, lanes].astype(F32) + rland[up, inner, lanes].astype(F32)
                total = total + rland[down, inner, lanes].astype(F32)
                x_hat = (ag[0, rows, lanes].astype(F32) - center) * inverse
                scaled = total * gain[mp, :, lanes]
                gi_out[rows, lanes] = ((scaled - plain - x_hat * hat) * inverse).astype(BF16)
        return carry

    lax.fori_loop(0, HALF // 64, in_step, 0)

    y_full(0, 1, 0).wait_recv()
    y_full(0, -1, 0).wait_recv()
    finish(0, [yland.at[0], yland.at[1]])

    @pl.when(c == x)
    def _():
        fin[c] = last[0]
        remote(last.at[0], fin.at[1 - c], f_s.at[0], f_r.at[1 - c], at_c).wait_recv()

    @pl.when(c != x)
    def _():
        copy_a.start()
        for h in range(2):
            remote(last.at[1], fin.at[h], f_s.at[1], f_r.at[h], at_x).wait_recv()
        copy_a.wait_send()

    for h in range(2):
        for k in range(3):
            gw_out[k, :, h * HDIM : (h + 1) * HDIM] = fin[h, k * HDIM : (k + 1) * HDIM, :].T

    copy_b.wait_send()
    for sign in (1, -1):
        for k in range(1, 8):
            gather(sign, k).wait_send()
            reduce(sign, k).wait_send()
        for s, dxh in ((1, 1), (1, 0), (0, 0)):
            y_half(s, sign, dxh).wait_send()
            y_full(s, sign, dxh).wait_send()
    for n in range(2):
        gp_copy(n).wait_send()
        exchange_x(n).wait_send()
        for k in range(1, 8):
            exchange_z(n, k).wait_send()
        for o in range(8):
            core_copy(n, o).wait_send()
    w_cross().wait_send()
    for sign in (1, -1):
        w_ring(sign, 0).wait_send()
        w_ring(sign, 1).wait_send()
        w_ring_far(sign).wait_send()
    for i in range(4):
        w_core(i).wait_send()
    for n in (0, 1, 2, 3, LAST):
        x_copy(n).wait_send()


def shards(tokens, ln_gain, projected, out_grad, w_joined):
    vmem = pltpu.VMEM
    dma = pltpu.SemaphoreType.DMA
    hbm = pl.BlockSpec(memory_space=pl.ANY)
    local = pl.BlockSpec(memory_space=pltpu.VMEM)
    grad_weight, grad_input = pl.pallas_call(
        kernel,
        out_shape=(
            jax.ShapeDtypeStruct((3, COLS, WIDTH), BF16),
            jax.ShapeDtypeStruct((SEQ, COLS), BF16),
        ),
        in_specs=[hbm, local, hbm, hbm, hbm],
        out_specs=(local, local),
        scratch_shapes=[
            vmem((8, SEQ, COLS), BF16),
            vmem((8, 3, COLS, WIDTH), BF16),
            vmem((8, 3, COLS, WIDTH), BF16),
            vmem((3, SEQ, WIDTH), BF16),
            vmem((SEQ, WIDTH), BF16),
            vmem((2, 3, SEQ, WIDTH), BF16),
            vmem((2, 2 * GCOLS, SEQ), BF16),
            vmem((8, SEQ, COLS), BF16),
            vmem((8, SEQ, COLS), BF16),
            vmem((14, HALF, COLS), BF16),
            vmem((2, 8, 2 * GCOLS, COLS), BF16),
            vmem((2, 8, GCOLS, COLS), BF16),
            vmem((8, GCOLS, COLS), BF16),
            vmem((8, GHALF, COLS), BF16),
            vmem((5, GCOLS, COLS), BF16),
            vmem((2, GCOLS, COLS), BF16),
            vmem((2, GCOLS, COLS), BF16),
            vmem((SEQ, LANES), F32),
            vmem((SEQ, LANES), F32),
            vmem((SEQ, LANES), F32),
            vmem((SEQ, LANES), F32),
            vmem((2, 8, LANES), F32),
            vmem((2, 8, LANES), F32),
            vmem((2, 8, LANES), F32),
            vmem((2, 8, 8, LANES), F32),
            dma((3,)),
            dma((8,)),
            dma((14,)), dma((14,)),
            dma((2,)), dma((2,)),
            dma((2, 8)), dma((2, 8)),
            dma((7,)), dma((7,)),
            dma((4,)), dma((4,)),
            dma((2,)), dma((2,)),
            dma((14,)), dma((14,)),
            dma((2, 8)), dma((2, 8)),
            dma((16,)), dma((16,)),
            dma((5,)), dma((5,)),
            dma((2,)), dma((2,)),
        ],
        compiler_params=pltpu.CompilerParams(
            collective_id=0, has_side_effects=True, vmem_limit_bytes=62 * 1024 * 1024
        ),
        cost_estimate=pl.CostEstimate(flops=11_000_000_000, bytes_accessed=14_000_000, transcendentals=600_000),
        name="parallel_block_backward",
    )(
        tokens,
        ln_gain.reshape(16, 1, COLS),
        jnp.transpose(projected, (1, 0, 2)),
        out_grad,
        jnp.transpose(w_joined, (1, 0, 2)),
    )
    return jnp.transpose(grad_weight, (1, 0, 2)).astype(F32), grad_input


def solution(mesh):
    in_specs = (P("dp", "mp"), P(), P("dp", None, "mp"), P("dp", "mp"), P(None, None, "mp"))
    out_specs = (P("dp", None, "mp"), P("dp", "mp"))
    return jax.shard_map(shards, mesh=mesh, in_specs=in_specs, out_specs=out_specs, check_vma=False)
```

```python
import functools

import jax
import jax.numpy as jnp
from jax import lax
from jax.experimental import pallas as pl
from jax.experimental.pallas import tpu as pltpu
from jax.sharding import PartitionSpec as P

MESH = pl.DeviceIdType.MESH
F32 = jnp.float32
BF16 = jnp.bfloat16

D = 6144
HDIM = 128
SEQ = 512
COLS = 384
WIDTH = 256
HALF = SEQ // 2
GCOLS = 3 * HDIM
GHALF = GCOLS // 2
SCALE = HDIM ** (-0.5)
LANES = 128
LAST = None

NT = (((1,), (1,)), ((), ()))
NN = (((1,), (0,)), ((), ()))
TN = (((0,), (0,)), ((), ()))


def slot(dz):
    return 7 if abs(dz) == 4 else (2 * abs(dz) - (1 if dz < 0 else 0))


def dot(left, right, dims):
    return lax.dot_general(left, right, dims, preferred_element_type=F32)


def add_into(dst, sources, rows, chunk=64):
    def body(i, carry):
        at = pl.ds(pl.multiple_of(i * chunk, chunk), chunk)
        total = dst[at, :].astype(F32)
        for source in sources:
            total = total + source[at, :].astype(F32)
        dst[at, :] = total.astype(BF16)
        return carry

    lax.fori_loop(0, rows // chunk, body, 0)


def pack_rows(acc, out, first):
    for i in range(4):
        part = acc[i * LANES : (i + 1) * LANES, :]
        out[first + i : first + i + 1, :] = jnp.sum(part.T, axis=0, keepdims=True)


def spread_rows(rows, out):
    for i in range(4):
        out[i * LANES : (i + 1) * LANES, :] = jnp.broadcast_to(rows[i : i + 1, :], (LANES, LANES)).T


def kernel(
    tok, gain, proj, og, w, gw_out, gi_out,
    ag, wv, wx, pv, ov, gp, gpt, norm, part, rland, gsum, cland, yland, yhalf, xland, fin, last,
    acc_a, acc_b, mean_b, inv_b, st_send, st_recv, sz_send, sz_recv,
    load_sem, w_sem, ag_s, ag_r, st_s, st_r, sz_s, sz_r, wx_s, wx_r, wc_s, wc_r, gp_s, gp_r,
    rs_s, rs_r, c_s, c_r, y_s, y_r, x_s, x_r, f_s, f_r,
):
    dp, mp = lax.axis_index("dp"), lax.axis_index("mp")
    y, xh, c = dp // 4, (dp // 2) % 2, dp % 2
    z, x = mp // 2, mp % 2

    def at_z(k):
        return (dp, ((z + k + 8) % 8) * 2 + x)

    def at_y(k):
        return (((y + k + 4) % 4) * 4 + xh * 2 + c, mp)

    sibling = y * 4 + xh * 2 + 1 - c
    at_c = (sibling, mp)
    at_x = (dp, z * 2 + 1 - x)
    at_xc = (sibling, z * 2 + 1 - x)
    at_xh = (y * 4 + (1 - xh) * 2 + c, mp)
    at_xo = (y * 4 + (1 - xh) * 2 + c, z * 2 + 1 - x)

    def remote(src, dst, send, recv, device):
        return pltpu.make_async_remote_copy(
            src_ref=src, dst_ref=dst, send_sem=send, recv_sem=recv, device_id=device, device_id_type=MESH
        )

    def zed(n):
        return (z + ((n + 1) // 2) * (1 - 2 * (n % 2)) + 8) % 8

    def w_rows(n, column):
        return w.at[:, pl.ds(pl.multiple_of((zed(n) * 2 + column) * COLS, COLS), COLS), :]

    loads = [
        pltpu.make_async_copy(tok, ag.at[0], load_sem.at[0]),
        pltpu.make_async_copy(proj, pv, load_sem.at[1]),
        pltpu.make_async_copy(og, ov, load_sem.at[2]),
    ]
    for load in loads:
        load.start()

    def w_load(n):
        return pltpu.make_async_copy(w_rows(n, x), wv.at[n], w_sem.at[n])

    barrier = pltpu.get_barrier_semaphore()
    peers = [at_z(k) for k in range(1, 8)] + [at_c, at_x, at_xc, at_xh, at_xo, at_y(1), at_y(-1)]
    for peer in peers:
        pl.semaphore_signal(barrier, inc=1, device_id=peer, device_id_type=MESH)
    pl.semaphore_wait(barrier, len(peers))

    def gather(sign, k):
        hop = (k - 1) // 2
        half = (0 if sign > 0 else 1) if k % 2 == 1 else (1 if sign > 0 else 0)
        rows = pl.ds(half * HALF, HALF)
        src = tok.at[rows] if hop == 0 else ag.at[slot(-sign * hop), rows]
        e = (0 if sign > 0 else 7) + k - 1
        return remote(src, ag.at[slot(-sign * (hop + 1)), rows], ag_s.at[e], ag_r.at[e], at_z(sign))

    def gather_event(k):
        for sign in (1, -1):
            gather(sign, k).wait_recv()
            if k <= 5:
                gather(sign, k + 2).start()

    gather(1, 1).start()
    gather(-1, 1).start()

    def w_place(d, core):
        return 2 * ((y - d + 4) % 4) + 1 - core

    def w_cross():
        n = w_place(0, c)
        partner = (y * 4 + ((xh + c) % 2) * 2 + c, z * 2 + 1 - x)
        return remote(w_rows(n, 1 - x), wx.at[n], wx_s.at[0], wx_r.at[0], partner)

    def w_ring(sign, part):
        n = w_place(0, c)
        e = (1 if sign > 0 else 2) + 4 * part
        rows = pl.ds(0 if (sign > 0) == (part == 0) else COLS // 2, COLS // 2)
        return remote(wx.at[n, :, rows], wx.at[n, :, rows], wx_s.at[e], wx_r.at[e], at_y(sign))

    def w_ring_far(sign):
        n = w_place(sign, c)
        e = 3 if sign > 0 else 4
        rows = pl.ds(0 if sign > 0 else COLS // 2, COLS // 2)
        return remote(wx.at[n, :, rows], wx.at[n, :, rows], wx_s.at[e], wx_r.at[e], at_y(sign))

    def w_core(i):
        n = w_place((0, 1, -1, 2)[i], c)
        return remote(wx.at[n], wx.at[n], wc_s.at[i], wc_r.at[i], at_c)

    w_cross().start()
    for n in (7, 6, 5, 4, 3, 2, 1, 0):
        w_load(n).start()

    def exchange_x(n):
        return remote(st_send.at[n], st_recv.at[n], st_s.at[n], st_r.at[n], at_x)

    def exchange_z(n, k):
        return remote(sz_send.at[n], sz_recv.at[n, k], sz_s.at[n, k], sz_r.at[n, k], at_z(k))

    loads[0].wait()
    for i in range(4):
        rows = slice(i * LANES, (i + 1) * LANES)
        tiles = [ag[0, rows, k * LANES : (k + 1) * LANES].astype(F32) for k in range(3)]
        sums = tiles[0] + tiles[1] + tiles[2]
        center = jnp.sum(sums, axis=1, keepdims=True) / COLS
        acc_a[rows, :] = sums
        acc_b[rows, :] = sum(jnp.square(tile - center) for tile in tiles)
    pack_rows(acc_a, st_send.at[0], 0)
    pack_rows(acc_b, st_send.at[0], 4)
    st_send[0, 0:4, :] = st_send[0, 0:4, :] / COLS
    exchange_x(0).start()
    gather(1, 2).start()
    gather(-1, 2).start()

    def gp_copy(h):
        lanes = pl.ds(h * HDIM, HDIM)
        return remote(gp.at[0, :, :, lanes], gp.at[1, :, :, lanes], gp_s.at[h], gp_r.at[h], at_x)

    def head(h):
        cols = slice(h * HDIM, (h + 1) * HDIM)
        queries, keys_all, values, upstream = pv[0, :, cols], pv[1, :, cols], pv[2, :, cols], ov[:, cols]
        key_grad = value_grad = None
        for q0 in range(0, SEQ, 256):
            qs = slice(q0, q0 + 256)
            scores = dot(keys_all, queries[qs], NT) * SCALE
            raised = jnp.exp(scores - jnp.max(scores, axis=0, keepdims=True))
            probs = raised / jnp.sum(raised, axis=0, keepdims=True)
            term = dot(probs.astype(BF16), upstream[qs], NN)
            value_grad = term if value_grad is None else value_grad + term
            prob_grad = dot(values, upstream[qs], NT)
            score_grad = probs * (prob_grad - jnp.sum(probs * prob_grad, axis=0, keepdims=True))
            score_low = score_grad.astype(BF16)
            term = dot(score_low, queries[qs], NN)
            key_grad = term if key_grad is None else key_grad + term
            gp[0, 0, qs, cols] = (dot(score_low, keys_all, TN) * SCALE).astype(BF16)
        gp[0, 1, :, cols] = (key_grad * SCALE).astype(BF16)
        gp[0, 2, :, cols] = value_grad.astype(BF16)
        gp_copy(h).start()

    def turn(s, h):
        for k in range(3):
            first = h * GCOLS + k * HDIM
            gpt[s, first : first + HDIM, :] = gp[s, k, :, h * HDIM : (h + 1) * HDIM].T

    loads[1].wait()
    loads[2].wait()
    head(0)

    exchange_x(0).wait_recv()
    mine, other = st_send[0], st_recv[0]
    center = (mine[0:4] + other[0:4]) * 0.5
    sz_send[0, 0:4, :] = center
    sz_send[0, 4:8, :] = mine[4:8] + other[4:8] + COLS * (
        jnp.square(mine[0:4] - center) + jnp.square(other[0:4] - center)
    )
    for k in range(1, 8):
        exchange_z(0, k).start()

    gather_event(1)
    w_cross().wait_recv()
    w_ring(1, 0).start()
    w_ring(-1, 0).start()
    w_core(0).start()

    head(1)

    gather_event(2)
    w_ring(1, 1).start()
    w_ring(-1, 1).start()
    turn(0, 0)
    turn(0, 1)
    gather_event(3)
    for sign in (1, -1):
        w_ring(sign, 0).wait_recv()
        w_ring_far(sign).start()

    for k in range(1, 8):
        exchange_z(0, k).wait_recv()
    centers = [sz_send[0, 0:4, :]] + [sz_recv[0, k, 0:4, :] for k in range(1, 8)]
    squares = [sz_send[0, 4:8, :]] + [sz_recv[0, k, 4:8, :] for k in range(1, 8)]
    center = sum(centers) * 0.125
    spread = (sum(squares) + (2 * COLS) * sum(jnp.square(one - center) for one in centers)) / D
    spread_rows(center, mean_b)
    spread_rows(lax.rsqrt(spread + 1e-06), inv_b)
    gather_event(4)

    acc_a[...] = jnp.zeros_like(acc_a)
    acc_b[...] = jnp.zeros_like(acc_b)

    def head_rows(core):
        return pl.ds(pl.multiple_of(core * GCOLS, GCOLS), GCOLS)

    def core_copy(s, o):
        return remote(gsum.at[s, o, head_rows(1 - c)], cland.at[s, o], c_s.at[s, o], c_r.at[s, o], at_c)

    def weight(s, n):
        o = ((zed(n) // 2 - y + 4) % 4) * 2 + (zed(n) + xh) % 2
        gsum[s, o] = dot(gpt[s], norm[n], NN).astype(BF16)
        core_copy(s, o).start()

    def x_copy(n):
        src = cland.at[1, 1] if n is LAST else cland.at[0, n * 2 + 1]
        n = 4 if n is LAST else n
        return remote(src, xland.at[n], x_s.at[n], x_r.at[n], at_xh)

    def x_event(n):
        dy = (zed(n) // 2 - y + 4) % 4

        @pl.when((zed(n) + xh) % 2 == 1)
        def _():
            core_copy(0, dy * 2 + 1).wait_recv()
            add_into(cland.at[0, dy * 2 + 1], [gsum.at[0, dy * 2 + 1, head_rows(c)]], GCOLS)
            x_copy(dy).start()

    def normalize(n):
        j = zed(n) * 2 + x

        def rows_step(r, carry):
            rows = pl.ds(pl.multiple_of(r * 64, 64), 64)
            center, inverse = mean_b[rows, :], inv_b[rows, :]
            for k in range(3):
                lanes = slice(k * LANES, (k + 1) * LANES)
                value = (ag[n, rows, lanes].astype(F32) - center) * inverse * gain[j, :, lanes]
                norm[n, rows, lanes] = value.astype(BF16)
            return carry

        lax.fori_loop(0, SEQ // 64, rows_step, 0)

    def weight_own(n, carry):
        normalize(n)
        weight(0, n)

        @pl.when(n > 4)
        def _():
            x_event(n - 1)

        return carry

    def x_step(n, carry):
        x_event(n)
        return carry

    def weight_cross(n, carry):
        weight(1, n)
        return carry

    def share(n):
        for k in range(3):
            term = dot(gp[0, k], wv[n, k], NT) + dot(gp[1, k], wx[n, k], NT)
            total = term if k == 0 else total + term
        part[n] = total.astype(BF16)

    def sums(n):
        j = zed(n) * 2 + x

        def rows_step(r, carry):
            rows = pl.ds(pl.multiple_of(r * 64, 64), 64)
            plain, hat = acc_a[rows, :], acc_b[rows, :]
            for k in range(3):
                lanes = slice(k * LANES, (k + 1) * LANES)
                piece = part[n, rows, lanes].astype(F32)
                plain = plain + piece * gain[j, :, lanes]
                hat = hat + piece * norm[n, rows, lanes].astype(F32)
            acc_a[rows, :] = plain
            acc_b[rows, :] = hat
            return carry

        lax.fori_loop(0, SEQ // 64, rows_step, 0)

    def share_near(i, carry):
        share(4 - i)
        sums(4 - i)
        return carry

    def sums_step(n, carry):
        sums(n)
        return carry

    def reduce(sign, k):
        dz = sign * (4 - k // 2)
        first = 1 if sign > 0 else 0
        half = first if k % 2 == 1 else 1 - first
        e = (0 if sign > 0 else 7) + k - 1
        return remote(
            part.at[slot(dz), pl.ds(half * HALF, HALF)], rland.at[e], rs_s.at[e], rs_r.at[e], at_z(sign)
        )

    def reduce_event(k):
        for sign in (1, -1):
            dz = sign * (4 - (k + 2) // 2)
            first = 1 if sign > 0 else 0
            half = first if k % 2 == 1 else 1 - first
            reduce(sign, k).wait_recv()
            e = (0 if sign > 0 else 7) + k - 1
            add_into(part.at[slot(dz), pl.ds(half * HALF, HALF)], [rland.at[e]], HALF)
            reduce(sign, k + 2).start()

    lax.fori_loop(0, 3, weight_own, 0)
    gather_event(5)
    w_ring(1, 1).wait_recv()
    w_ring(-1, 1).wait_recv()
    w_core(1).start()
    w_core(2).start()
    lax.fori_loop(3, 5, weight_own, 0)
    gp_copy(0).wait_recv()
    gp_copy(1).wait_recv()
    lax.fori_loop(0, 4, x_step, 0)
    turn(1, 0)
    turn(1, 1)
    gather_event(6)
    lax.fori_loop(5, 7, weight_own, 0)
    lax.fori_loop(0, 5, weight_cross, 0)

    w_ring_far(1).wait_recv()
    w_ring_far(-1).wait_recv()
    w_core(3).start()
    for n in range(8):
        w_load(n).wait()
    for i in range(4):
        w_core(i).wait_recv()
    share(7)
    reduce(1, 1).start()
    reduce(-1, 1).start()
    share(6)
    reduce(1, 2).start()
    share(5)
    reduce(-1, 2).start()
    gather_event(7)
    normalize(7)
    lax.fori_loop(5, 8, weight_cross, 0)
    weight(0, 7)

    def core_add(s, dy, dxh, more=()):
        o = dy * 2 + dxh
        core_copy(s, o).wait_recv()
        add_into(cland.at[s, o], [gsum.at[s, o, head_rows(c)], *more], GCOLS)

    def y_place(s, sign, dxh):
        return s * 4 + dxh * 2 + (0 if sign > 0 else 1)

    def y_half(s, sign, dxh):
        n = y_place(s, sign, dxh)
        half = 0 if sign > 0 else 1
        src = cland.at[s, 4 + dxh, pl.ds(half * GHALF, GHALF)]
        return remote(src, yhalf.at[n], y_s.at[n], y_r.at[n], at_y(sign))

    def y_full(s, sign, dxh):
        n = y_place(s, sign, dxh)
        src = cland.at[s, (2 if sign > 0 else 6) + dxh]
        return remote(src, yland.at[n], y_s.at[8 + n], y_r.at[8 + n], at_y(sign))

    def y_pass(s, dxh):
        for sign, dy, half in ((1, 1, 0), (-1, 3, 1)):
            n = y_place(s, sign, dxh)
            y_half(s, sign, dxh).wait_recv()
            add_into(cland.at[s, dy * 2 + dxh, pl.ds(half * GHALF, GHALF)], [yhalf.at[n]], GHALF)
            y_full(s, sign, dxh).start()

    core_add(1, 2, 1)
    y_half(1, 1, 1).start()
    y_half(1, -1, 1).start()
    lax.fori_loop(6, 8, x_step, 0)
    lax.fori_loop(5, 8, sums_step, 0)
    reduce_event(1)
    lax.fori_loop(0, 2, share_near, 0)
    reduce_event(2)
    core_add(1, 2, 0)
    y_half(1, 1, 0).start()
    y_half(1, -1, 0).start()
    core_add(1, 1, 1)
    core_add(1, 3, 1)
    y_pass(1, 1)
    reduce_event(3)
    lax.fori_loop(2, 5, share_near, 0)

    pack_rows(acc_a, st_send.at[1], 0)
    pack_rows(acc_b, st_send.at[1], 4)
    exchange_x(1).start()

    reduce_event(4)
    core_add(1, 1, 0)
    core_add(1, 3, 0)
    y_pass(1, 0)
    exchange_x(1).wait_recv()
    sz_send[1] = st_send[1] + st_recv[1]
    for k in range(1, 8):
        exchange_z(1, k).start()
    core_add(1, 0, 1)
    core_add(1, 0, 0)

    y_full(1, 1, 1).wait_recv()
    y_full(1, -1, 1).wait_recv()
    add_into(cland.at[1, 1], [yland.at[6], yland.at[7]], GCOLS)
    x_copy(LAST).start()
    x_copy(2).wait_recv()
    core_add(0, 2, 0, [xland.at[2]])
    y_half(0, 1, 0).start()
    y_half(0, -1, 0).start()
    reduce_event(5)

    for dy in (1, 3):
        x_copy(dy).wait_recv()
        core_add(0, dy, 0, [xland.at[dy]])

    for k in range(1, 8):
        exchange_z(1, k).wait_recv()
    total = (sz_send[1] + sum(sz_recv[1, k] for k in range(1, 8))) / D
    spread_rows(total[0:4], acc_a)
    spread_rows(total[4:8], acc_b)

    owner_b = (y * 4 + xh * 2 + x, z * 2 + 1 - x)
    copy_b = remote(last.at[1], fin.at[c], f_s.at[1], f_r.at[c], owner_b)
    copy_a = remote(last.at[0], fin.at[c], f_s.at[0], f_r.at[c], at_c)

    def finish(s, sources):
        def step(r, carry):
            rows = pl.ds(pl.multiple_of(r * 64, 64), 64)
            total = cland[s, 0, rows, :].astype(F32)
            for source in sources:
                total = total + source[rows, :].astype(F32)
            last[s, rows, :] = total.astype(BF16)
            return carry

        lax.fori_loop(0, GCOLS // 64, step, 0)

    y_full(1, 1, 0).wait_recv()
    y_full(1, -1, 0).wait_recv()
    x_copy(LAST).wait_recv()
    finish(1, [yland.at[4], yland.at[5], xland.at[4]])
    copy_b.start()
    y_pass(0, 0)
    x_copy(0).wait_recv()
    core_add(0, 0, 0, [xland.at[0]])

    y_full(0, 1, 0).wait_recv()
    y_full(0, -1, 0).wait_recv()
    finish(0, [yland.at[0], yland.at[1]])

    @pl.when(c != x)
    def _():
        copy_a.start()

    for k in (6, 7):
        reduce(1, k).wait_recv()
        reduce(-1, k).wait_recv()

    def in_step(r, carry):
        center, inverse = None, None
        for half in range(2):
            rows = pl.ds(pl.multiple_of(half * HALF + r * 64, 64), 64)
            inner = pl.ds(pl.multiple_of(r * 64, 64), 64)
            up, down = (5, 13) if half == 0 else (6, 12)
            center, inverse = mean_b[rows, :], inv_b[rows, :]
            plain, hat = acc_a[rows, :], acc_b[rows, :]
            for k in range(3):
                lanes = slice(k * LANES, (k + 1) * LANES)
                total = part[0, rows, lanes].astype(F32) + rland[up, inner, lanes].astype(F32)
                total = total + rland[down, inner, lanes].astype(F32)
                x_hat = (ag[0, rows, lanes].astype(F32) - center) * inverse
                scaled = total * gain[mp, :, lanes]
                gi_out[rows, lanes] = ((scaled - plain - x_hat * hat) * inverse).astype(BF16)
        return carry

    lax.fori_loop(0, HALF // 64, in_step, 0)

    @pl.when(c == x)
    def _():
        fin[c] = last[0]
        remote(last.at[0], fin.at[1 - c], f_s.at[0], f_r.at[1 - c], at_c).wait_recv()

    @pl.when(c != x)
    def _():
        for h in range(2):
            remote(last.at[1], fin.at[h], f_s.at[1], f_r.at[h], at_x).wait_recv()
        copy_a.wait_send()

    for h in range(2):
        for k in range(3):
            gw_out[k, :, h * HDIM : (h + 1) * HDIM] = fin[h, k * HDIM : (k + 1) * HDIM, :].T

    copy_b.wait_send()
    for sign in (1, -1):
        for k in range(1, 8):
            gather(sign, k).wait_send()
            reduce(sign, k).wait_send()
        for s, dxh in ((1, 1), (1, 0), (0, 0)):
            y_half(s, sign, dxh).wait_send()
            y_full(s, sign, dxh).wait_send()
    for n in range(2):
        gp_copy(n).wait_send()
        exchange_x(n).wait_send()
        for k in range(1, 8):
            exchange_z(n, k).wait_send()
        for o in range(8):
            core_copy(n, o).wait_send()
    w_cross().wait_send()
    for sign in (1, -1):
        w_ring(sign, 0).wait_send()
        w_ring(sign, 1).wait_send()
        w_ring_far(sign).wait_send()
    for i in range(4):
        w_core(i).wait_send()
    for n in (0, 1, 2, 3, LAST):
        x_copy(n).wait_send()


def shards(tokens, ln_gain, projected, out_grad, w_joined):
    vmem = pltpu.VMEM
    dma = pltpu.SemaphoreType.DMA
    hbm = pl.BlockSpec(memory_space=pl.ANY)
    local = pl.BlockSpec(memory_space=pltpu.VMEM)
    grad_weight, grad_input = pl.pallas_call(
        kernel,
        out_shape=(
            jax.ShapeDtypeStruct((3, COLS, WIDTH), BF16),
            jax.ShapeDtypeStruct((SEQ, COLS), BF16),
        ),
        in_specs=[hbm, local, hbm, hbm, hbm],
        out_specs=(local, local),
        scratch_shapes=[
            vmem((8, SEQ, COLS), BF16),
            vmem((8, 3, COLS, WIDTH), BF16),
            vmem((8, 3, COLS, WIDTH), BF16),
            vmem((3, SEQ, WIDTH), BF16),
            vmem((SEQ, WIDTH), BF16),
            vmem((2, 3, SEQ, WIDTH), BF16),
            vmem((2, 2 * GCOLS, SEQ), BF16),
            vmem((8, SEQ, COLS), BF16),
            vmem((8, SEQ, COLS), BF16),
            vmem((14, HALF, COLS), BF16),
            vmem((2, 8, 2 * GCOLS, COLS), BF16),
            vmem((2, 8, GCOLS, COLS), BF16),
            vmem((8, GCOLS, COLS), BF16),
            vmem((8, GHALF, COLS), BF16),
            vmem((5, GCOLS, COLS), BF16),
            vmem((2, GCOLS, COLS), BF16),
            vmem((2, GCOLS, COLS), BF16),
            vmem((SEQ, LANES), F32),
            vmem((SEQ, LANES), F32),
            vmem((SEQ, LANES), F32),
            vmem((SEQ, LANES), F32),
            vmem((2, 8, LANES), F32),
            vmem((2, 8, LANES), F32),
            vmem((2, 8, LANES), F32),
            vmem((2, 8, 8, LANES), F32),
            dma((3,)),
            dma((8,)),
            dma((14,)), dma((14,)),
            dma((2,)), dma((2,)),
            dma((2, 8)), dma((2, 8)),
            dma((7,)), dma((7,)),
            dma((4,)), dma((4,)),
            dma((2,)), dma((2,)),
            dma((14,)), dma((14,)),
            dma((2, 8)), dma((2, 8)),
            dma((16,)), dma((16,)),
            dma((5,)), dma((5,)),
            dma((2,)), dma((2,)),
        ],
        compiler_params=pltpu.CompilerParams(
            collective_id=0, has_side_effects=True, vmem_limit_bytes=62 * 1024 * 1024
        ),
        cost_estimate=pl.CostEstimate(flops=11_000_000_000, bytes_accessed=14_000_000, transcendentals=600_000),
        name="parallel_block_backward",
    )(
        tokens,
        ln_gain.reshape(16, 1, COLS),
        jnp.transpose(projected, (1, 0, 2)),
        out_grad,
        jnp.transpose(w_joined, (1, 0, 2)),
    )
    return jnp.transpose(grad_weight, (1, 0, 2)).astype(F32), grad_input


def solution(mesh):
    in_specs = (P("dp", "mp"), P(), P("dp", None, "mp"), P("dp", "mp"), P(None, None, "mp"))
    out_specs = (P("dp", None, "mp"), P("dp", "mp"))
    return jax.shard_map(shards, mesh=mesh, in_specs=in_specs, out_specs=out_specs, check_vma=False)
```
